128 devices in a mesh: blk: 32 (over x_lo, z, y), chan: 4 (over x_hi, core).
Axes of the slice: x: 4 (x_hi: 2, x_lo: 2; x = x_hi * 2 + x_lo), y: 4, z: 4, core: 2. Of those that a mesh axis runs over, the one named last changes fastest.
Arguments:
- pair_rep: bfloat16 [512, 512, 128], P('blk'), may hold values from -6 to 6
- proj_weight: bfloat16 [2, 4, 128, 128], P(None, None, None, 'chan'), may hold values from -0.5 to 0.5
- gate_weight: bfloat16 [2, 128, 128], replicated, may hold values from -0.5 to 0.5
- out_weight: bfloat16 [2, 128, 128], P(None, 'chan'), may hold values from -0.5 to 0.5
- in_gain: float32 [2, 128], replicated, may hold values from 0.1 to 1.9
- out_gain: float32 [2, 128], P(None, 'chan'), may hold values from 0.1 to 1.9
Outputs:
- pair_out: bfloat16 [512, 512, 128], P('blk', 'chan')
The draws below stay inside these ranges and needn't reach their ends.
All inputs are finite; a program needn't handle non-finite values.
Results may differ from the reference program's by a relative error of at most 0.02.
Values may be sent and summed in bfloat16 or wider, within the bound.
No kernel may reach another device: no remote copies, remote signals or barrier semaphores. Data moves between devices by JAX's collectives and lax.ppermute only.
A program may use at most 128 MiB of HBM per device.

```python
import jax
import jax.numpy as jnp
from jax import lax

PAIR_CH = 128
HIDDEN_SIZE = 128
RESIDUES = 512


def block_levels(key, dims, pieces, smallest, largest):
    level = 1.0
    for axis_at, shards_of in pieces:
        draws = jax.random.uniform(jax.random.fold_in(jax.random.fold_in(key, 6), axis_at), (shards_of,), jnp.float32, smallest / len(pieces), largest / len(pieces))
        level = level * jnp.repeat(jnp.exp(draws), dims[axis_at] // shards_of).reshape((-1,) + (1,) * (len(dims) - 1 - axis_at))
    return level


def noise(stream_key, shape, scale, most, split=(), dtype=jnp.bfloat16):
    level = block_levels(stream_key, shape, split, -0.22, 0.18) if split else 1.0
    entries = jax.random.normal(stream_key, shape, jnp.float32) * scale * level
    return jnp.minimum(jnp.maximum(entries, -most), most).astype(dtype)


def setup_inputs(seed: int = 0) -> dict:
    streams_of = jax.random.split(jax.random.key(seed), 7)
    return {
        "pair_rep": noise(streams_of[0], (RESIDUES, RESIDUES, PAIR_CH), 1.0, 6.0, ((0, 32),)),
        "proj_weight": noise(streams_of[1], (2, 4, PAIR_CH, HIDDEN_SIZE), PAIR_CH ** -0.5, 0.5, ((3, 4),)),
        "gate_weight": noise(streams_of[2], (2, PAIR_CH, PAIR_CH), PAIR_CH ** -0.5, 0.5),
        "out_weight": noise(streams_of[3], (2, HIDDEN_SIZE, PAIR_CH), HIDDEN_SIZE ** -0.5, 0.5, ((1, 4),)),
        "in_gain": jnp.clip(1.0 + 0.18 * jax.random.normal(streams_of[4], (2, PAIR_CH), jnp.float32), 0.1, 1.9),
        "out_gain": jnp.clip(1.0 + 0.18 * jax.random.normal(streams_of[5], (2, HIDDEN_SIZE), jnp.float32), 0.1, 1.9),
    }


epsilon = 1e-05

def cell_norm(values, gain):
    mean = lax.optimization_barrier(jnp.mean(values, -1, keepdims=True))
    square = lax.optimization_barrier(jnp.mean(values * values, -1, keepdims=True))
    return (values - mean) * lax.rsqrt(square - mean * mean + epsilon) * gain

def update_step(pair_rep, section, proj_weight, gate_weight, out_weight, in_gain, out_gain):
    normed = cell_norm(pair_rep.astype(jnp.float32), in_gain[section]).astype(jnp.bfloat16)
    flat = normed.reshape(-1, PAIR_CH)
    parts = [jnp.dot(flat, proj_weight[section, which], preferred_element_type=jnp.float32).reshape(RESIDUES, RESIDUES, HIDDEN_SIZE) for which in range(4)]
    left_part = (parts[0] * jax.nn.sigmoid(parts[1])).astype(jnp.bfloat16)
    right_part = (parts[2] * jax.nn.sigmoid(parts[3])).astype(jnp.bfloat16)
    gating = jax.nn.sigmoid(jnp.dot(flat, gate_weight[section], preferred_element_type=jnp.float32)).reshape(RESIDUES, RESIDUES, PAIR_CH)
    left_full = jnp.transpose(left_part, (2, 0, 1)).astype(jnp.float32)
    right_full = jnp.transpose(right_part, (2, 0, 1)).astype(jnp.float32)
    if section == 0:
        product = jnp.einsum('cik,cjk->cij', left_full, right_full, precision=lax.Precision.HIGHEST)
    else:
        product = jnp.einsum('cki,ckj->cij', left_full, right_full, precision=lax.Precision.HIGHEST)
    hidden_n = cell_norm(jnp.transpose(product, (1, 2, 0)), out_gain[section]).astype(jnp.bfloat16)
    update = jnp.dot(hidden_n.reshape(-1, HIDDEN_SIZE), out_weight[section], preferred_element_type=jnp.float32).reshape(RESIDUES, RESIDUES, PAIR_CH)
    return (pair_rep.astype(jnp.float32) + gating * update).astype(jnp.bfloat16)

def reference(pair_rep, proj_weight, gate_weight, out_weight, in_gain, out_gain):
    middle = update_step(pair_rep, 0, proj_weight, gate_weight, out_weight, in_gain, out_gain)
    return update_step(middle, 1, proj_weight, gate_weight, out_weight, in_gain, out_gain)
```

```python
import functools

import jax
import jax.numpy as jnp
from jax import lax
from jax.experimental import pallas as pl
from jax.experimental.pallas import tpu as pltpu
from jax.sharding import PartitionSpec as P

epsilon = 1e-05
F32 = jnp.float32
BF16 = jnp.bfloat16
VMEM_LIMIT = 48 * 1024 * 1024


def params():
    return pltpu.CompilerParams(vmem_limit_bytes=VMEM_LIMIT)


def cost(flops, moved):
    return pl.CostEstimate(flops=flops, bytes_accessed=moved, transcendentals=0)


def sig(x):
    return 0.5 + 0.5 * jnp.tanh(0.5 * x)


def dot(a, b, ca, cb):
    return lax.dot_general(a, b, (((ca,), (cb,)), ((), ())), preferred_element_type=F32)


def centering(n):
    eye = lax.broadcasted_iota(jnp.int32, (n, n), 0) == lax.broadcasted_iota(jnp.int32, (n, n), 1)
    return (jnp.where(eye, 1.0, 0.0) - 1.0 / n).astype(BF16)


def norm_last(x, gain):
    n = x.shape[-1]
    d = dot(x, centering(n), 1, 0)
    var = dot((d * d).astype(BF16), jnp.full((n, n), 1.0 / n, BF16), 1, 0)
    return (d * lax.rsqrt(var + epsilon) * gain).astype(BF16)


def project_kernel(x_ref, w_ref, gain_ref, out_ref, tmp):
    rows, cols, ch = x_ref.shape
    share = out_ref.shape[0]
    gain = gain_ref[...]
    for i in range(rows):
        normed = norm_last(x_ref[i], gain)
        parts = dot(w_ref[...], normed, 1, 1)
        left = parts[:share] * sig(parts[share : 2 * share])
        right = parts[2 * share : 3 * share] * sig(parts[3 * share :])
        tmp[0, pl.ds(i, share, stride=rows), :] = left
        tmp[1, pl.ds(i, share, stride=rows), :] = right
    for s in range(2):
        out_ref[:, s] = tmp[s].reshape(share, rows, cols).astype(BF16)


def project(x, w, gain, share):
    rows, width, ch = x.shape
    cols = 128
    return pl.pallas_call(
        project_kernel,
        grid=(width // cols,),
        in_specs=[
            pl.BlockSpec((rows, cols, ch), lambda t: (0, t, 0)),
            pl.BlockSpec(w.shape, lambda t: (0, 0)),
            pl.BlockSpec(gain.shape, lambda t: (0, 0)),
        ],
        out_specs=pl.BlockSpec((share, 2, rows, cols), lambda t: (0, 0, 0, t)),
        out_shape=jax.ShapeDtypeStruct((share, 2, rows, width), BF16),
        scratch_shapes=[pltpu.VMEM((2, share * rows, cols), F32)],
        compiler_params=params(),
        name="project_rows",
    )(x, w, gain)


def gate_kernel(x_ref, w_ref, gain_ref, out_ref):
    rows, cols, ch = x_ref.shape
    normed = norm_last(x_ref[...].reshape(rows * cols, ch), gain_ref[...])
    out_ref[...] = sig(dot(normed, w_ref[...], 1, 0)).reshape(rows, cols, ch)


def gates(x, w, gain):
    rows, cols, ch = x.shape
    return pl.pallas_call(
        gate_kernel,
        out_shape=jax.ShapeDtypeStruct(x.shape, F32),
        compiler_params=params(),
        cost_estimate=cost(6 * rows * cols * ch * ch, 6 * rows * cols * ch),
        name="gate_rows",
    )(x, w, gain)


def outgoing_kernel(x_ref, out_ref):
    blocks, _, rows, n = x_ref.shape
    tiles, cols = out_ref.shape[1], out_ref.shape[3]
    left = x_ref[:, 0].reshape(blocks * rows, n)
    per = cols // rows
    for q in range(tiles):
        right = x_ref[q * per : (q + 1) * per, 1].reshape(cols, n)
        out_ref[:, q] = dot(left, right, 1, 1).reshape(blocks, rows, cols).astype(BF16)


def outgoing(x, tiles):
    blocks, _, rows, n = x.shape
    return pl.pallas_call(
        outgoing_kernel,
        out_shape=jax.ShapeDtypeStruct((blocks, tiles, rows, n // tiles), BF16),
        compiler_params=params(),
        name="outgoing_product",
    )(x)


def incoming_kernel(x_ref, out_ref):
    blocks, tiles, _, rows, cols = x_ref.shape
    per = cols // rows
    rights = [x_ref[:, q, 1].reshape(blocks * rows, cols) for q in range(tiles)]
    right = jnp.concatenate(rights, axis=1)
    for p in range(tiles):
        left = x_ref[:, p, 0].reshape(blocks * rows, cols)
        product = dot(left, right, 0, 0).astype(BF16)
        for q in range(tiles):
            out_ref[p * per : (p + 1) * per, q] = product[:, q * cols : (q + 1) * cols].reshape(per, rows, cols)


def incoming(x):
    blocks, tiles, _, rows, cols = x.shape
    return pl.pallas_call(
        incoming_kernel,
        out_shape=jax.ShapeDtypeStruct((blocks, tiles, rows, cols), BF16),
        compiler_params=params(),
        name="incoming_product",
    )(x)


def normalized_products(p_ref, tmp):
    ch, rows, cols = p_ref.shape
    p = p_ref[...].astype(F32)
    d = p - jnp.sum(p, 0, keepdims=True) * (1.0 / ch)
    var = jnp.sum(d * d, 0, keepdims=True) * (1.0 / ch)
    tmp[...] = (d * lax.rsqrt(var + epsilon)).reshape(ch * rows, cols)


def middle_kernel(p_ref, pair_ref, gate_ref, ow_ref, w_ref, gain_ref, mid_ref, out_ref, tmp, tmp2):
    ch, rows, cols = p_ref.shape
    normalized_products(p_ref, tmp)
    gain = gain_ref[...]
    for i in range(rows):
        hidden = tmp[pl.ds(i, ch, stride=rows), :].astype(BF16)
        update = dot(hidden, ow_ref[...], 0, 0)
        mid = (pair_ref[i].astype(F32) + gate_ref[i] * update).astype(BF16)
        mid_ref[i] = mid
        parts = dot(w_ref[...], norm_last(mid, gain), 1, 1)
        tmp2[0, pl.ds(i, ch, stride=rows), :] = parts[:ch] * sig(parts[ch : 2 * ch])
        tmp2[1, pl.ds(i, ch, stride=rows), :] = parts[2 * ch : 3 * ch] * sig(parts[3 * ch :])
    for s in range(2):
        out_ref[:, s] = tmp2[s].reshape(ch, rows, cols).astype(BF16)


def middle_step(p, pair, gate, ow, w, gain):
    ch, rows, cols = p.shape
    return pl.pallas_call(
        middle_kernel,
        out_shape=(
            jax.ShapeDtypeStruct(pair.shape, BF16),
            jax.ShapeDtypeStruct((ch, 2, rows, cols), BF16),
        ),
        scratch_shapes=[pltpu.VMEM((ch * rows, cols), F32), pltpu.VMEM((2, ch * rows, cols), F32)],
        compiler_params=params(),
        name="middle_step",
    )(p, pair, gate, ow, w, gain)


def last_kernel(p_ref, mid_ref, gate_ref, ow_ref, out_ref, tmp):
    ch, rows, cols = p_ref.shape
    normalized_products(p_ref, tmp)
    for i in range(rows):
        hidden = tmp[pl.ds(i, ch, stride=rows), :].astype(BF16)
        update = dot(hidden, ow_ref[...], 0, 0)
        out_ref[i] = (mid_ref[i].astype(F32) + gate_ref[i] * update).astype(BF16)


def last_step(p, mid, gate, ow):
    ch, rows, cols = p.shape
    return pl.pallas_call(
        last_kernel,
        out_shape=jax.ShapeDtypeStruct(mid.shape, BF16),
        scratch_shapes=[pltpu.VMEM((ch * rows, cols), F32)],
        compiler_params=params(),
        name="last_step",
    )(p, mid, gate, ow)


def on_device(pair_rep, proj_weight, gate_weight, out_weight, in_gain, out_gain):
    rows, width, ch = pair_rep.shape
    tiles = lax.axis_size("chan")
    blocks = lax.axis_size("blk")
    share = proj_weight.shape[3]
    cols = width // tiles
    everywhere = ("blk", "chan")

    turned = jnp.transpose(proj_weight, (0, 1, 3, 2))
    mine = turned[0].reshape(4 * share, ch)
    scaled = (out_weight.astype(F32) * out_gain[:, :, None]).astype(BF16)
    packed = jnp.concatenate([turned[1].reshape(4 * share, ch), scaled.reshape(2 * share, ch)], 0)
    whole = lax.all_gather(packed, "chan", axis=0, tiled=False)

    def by_device(v):
        return jnp.moveaxis(v, 0, -2).reshape(v.shape[1:-2] + (share * tiles, ch))

    weights_in = by_device(whole[:, : 4 * share].reshape(tiles, 4, share, ch)).reshape(4 * share * tiles, ch)
    weights_out = by_device(whole[:, 4 * share :].reshape(tiles, 2, share, ch))

    halves = project(pair_rep, mine, in_gain[0:1], share)
    halves = lax.all_to_all(halves, "blk", 0, 0, tiled=True)
    own = lax.dynamic_slice_in_dim(pair_rep, lax.axis_index("chan") * cols, cols, 1)
    gate = gates(own, gate_weight[0], in_gain[0:1])

    product = outgoing(halves, tiles).reshape(blocks * tiles, rows, cols)
    product = lax.all_to_all(product, everywhere, 0, 0, tiled=True)
    mid, halves = middle_step(product, own, gate, weights_out[0], weights_in, in_gain[1:2])
    halves = lax.all_to_all(halves, everywhere, 0, 0, tiled=True)
    gate = gates(mid, gate_weight[1], in_gain[1:2])

    product = incoming(halves.reshape(blocks, tiles, 2, rows, cols)).reshape(blocks * tiles, rows, cols)
    product = lax.all_to_all(product, everywhere, 0, 0, tiled=True)
    return last_step(product, mid, gate, weights_out[1])


def solution(mesh):
    placed = (
        P("blk", None, None),
        P(None, None, None, "chan"),
        P(),
        P(None, "chan", None),
        P(),
        P(None, "chan"),
    )
    return jax.shard_map(
        on_device, mesh=mesh, in_specs=placed, out_specs=P("blk", "chan", None), check_vma=False
    )
```

```python
import jax
import jax.numpy as jnp
from jax import lax
from jax.experimental import pallas as pl
from jax.experimental.pallas import tpu as pltpu
from jax.sharding import PartitionSpec as P

epsilon = 1e-05
F32 = jnp.float32
BF16 = jnp.bfloat16
WHOLE = pl.BlockSpec(memory_space=pltpu.VMEM)


def params(mib):
    return pltpu.CompilerParams(vmem_limit_bytes=mib * 1024 * 1024)


def cost(flops, moved):
    return pl.CostEstimate(flops=flops, bytes_accessed=moved, transcendentals=0)


def dot(a, b, ca, cb):
    return lax.dot_general(a, b, (((ca,), (cb,)), ((), ())), preferred_element_type=F32)


def project_kernel(x_ref, w_ref, gain_ref, out_ref, tmp):
    rows, cols, ch = x_ref.shape
    share = out_ref.shape[0]
    weights = (w_ref[0].reshape(4 * share, ch).astype(F32) * gain_ref[0:1]).astype(BF16)
    x = jnp.concatenate([x_ref[i].T for i in range(rows)], 1).astype(F32)
    centered = x - jnp.sum(x, 0, keepdims=True) * (1.0 / ch)
    var = jnp.sum(centered * centered, 0, keepdims=True) * (1.0 / ch)
    scale = jnp.broadcast_to(0.5 * lax.rsqrt(var + epsilon), (share, rows * cols))
    parts = dot(weights, centered.astype(BF16), 1, 0)
    for i in range(rows):
        lanes = slice(i * cols, (i + 1) * cols)
        for s in range(2):
            value = parts[2 * s * share : (2 * s + 1) * share, lanes] * scale[:, lanes]
            gate = jnp.tanh(parts[(2 * s + 1) * share : (2 * s + 2) * share, lanes] * scale[:, lanes])
            tmp[s, pl.ds(i, share, stride=rows), :] = value + value * gate
    for s in range(2):
        out_ref[:, s] = tmp[s].reshape(share, rows, cols).astype(BF16)


def project(x, w, gain, cols):
    rows, width, ch = x.shape
    share = w.shape[2]
    return pl.pallas_call(
        project_kernel,
        grid=(width // cols,),
        in_specs=[pl.BlockSpec((rows, cols, ch), lambda t: (0, t, 0)), WHOLE, WHOLE],
        out_specs=pl.BlockSpec((share, 2, rows, cols), lambda t: (0, 0, 0, t)),
        out_shape=jax.ShapeDtypeStruct((share, 2, rows, width), BF16),
        scratch_shapes=[pltpu.VMEM((2, share * rows, cols), F32)],
        compiler_params=params(60),
        name="project_rows",
    )(x, w, gain)


def norm_down(x, gain):
    ch = x.shape[0]
    centered = x - jnp.sum(x, 0, keepdims=True) * (1.0 / ch)
    var = jnp.sum(centered * centered, 0, keepdims=True) * (1.0 / ch)
    out = centered * lax.rsqrt(var + epsilon)
    return (out if gain is None else out * gain).astype(BF16)


def gate_of(x, w_ref, gain_ref, s):
    w = (w_ref[s].astype(F32).T * gain_ref[s : s + 1]).astype(BF16)
    return 0.5 + 0.5 * jnp.tanh(0.5 * dot(w, norm_down(x, None), 1, 0))


def first_gate_kernel(x_ref, w_ref, gain_ref, turned_ref, gate_ref):
    rows, cols, ch = x_ref.shape
    turned = jnp.concatenate([x_ref[i].astype(F32).T for i in range(rows)], 1)
    turned_ref[...] = turned.astype(BF16)
    gate_ref[...] = gate_of(turned, w_ref, gain_ref, 0)


def first_gate(x, w, gain):
    rows, cols, ch = x.shape
    return pl.pallas_call(
        first_gate_kernel,
        out_shape=(
            jax.ShapeDtypeStruct((ch, rows * cols), BF16),
            jax.ShapeDtypeStruct((ch, rows * cols), F32),
        ),
        compiler_params=params(32),
        cost_estimate=cost(2 * rows * cols * ch * ch, 8 * rows * cols * ch),
        name="first_gate",
    )(x, w, gain)


def second_gate_kernel(x_ref, w_ref, gain_ref, gate_ref):
    gate_ref[...] = gate_of(x_ref[...].astype(F32), w_ref, gain_ref, 1)


def second_gate(x, w, gain):
    return pl.pallas_call(
        second_gate_kernel,
        out_shape=jax.ShapeDtypeStruct(x.shape, F32),
        compiler_params=params(32),
        cost_estimate=cost(2 * x.size * x.shape[0], 6 * x.size),
        name="second_gate",
    )(x, w, gain)


def outgoing_kernel(x_ref, out_ref):
    blocks, _, rows, n = x_ref.shape
    tiles, cols = out_ref.shape[1], out_ref.shape[3]
    left = x_ref[:, 0].reshape(blocks * rows, n)
    per = cols // rows
    for q in range(tiles):
        right = x_ref[q * per : (q + 1) * per, 1].reshape(cols, n)
        out_ref[:, q] = dot(left, right, 1, 1).reshape(blocks, rows, cols).astype(BF16)


def outgoing(x, tiles):
    blocks, _, rows, n = x.shape
    return pl.pallas_call(
        outgoing_kernel,
        out_shape=jax.ShapeDtypeStruct((blocks, tiles, rows, n // tiles), BF16),
        compiler_params=params(32),
        name="outgoing_product",
    )(x)


def incoming_kernel(x_ref, out_ref):
    blocks, tiles, _, rows, cols = x_ref.shape
    per = cols // rows
    rights = [x_ref[:, q, 1].reshape(blocks * rows, cols) for q in range(tiles)]
    right = jnp.concatenate(rights, axis=1)
    for p in range(tiles):
        left = x_ref[:, p, 0].reshape(blocks * rows, cols)
        product = dot(left, right, 0, 0).astype(BF16)
        for q in range(tiles):
            out_ref[p * per : (p + 1) * per, q] = product[:, q * cols : (q + 1) * cols].reshape(per, rows, cols)


def incoming(x):
    blocks, tiles, _, rows, cols = x.shape
    return pl.pallas_call(
        incoming_kernel,
        out_shape=jax.ShapeDtypeStruct((blocks, tiles, rows, cols), BF16),
        compiler_params=params(32),
        name="incoming_product",
    )(x)


def update_of(p_ref, whole_ref, s, tmp):
    ch, rows, cols = p_ref.shape
    tiles = whole_ref.shape[0]
    share = ch // tiles
    p = p_ref[...].astype(F32)
    tmp[...] = p.reshape(ch * rows, cols)
    mean = jnp.sum(p, 0) * (1.0 / ch)
    square = jnp.sum(p * p, 0) * (1.0 / ch)
    scale = lax.rsqrt(square - mean * mean + epsilon)
    weights = jnp.concatenate(
        [whole_ref[q, (4 + s) * share : (5 + s) * share] for q in range(tiles)], 0
    )
    columns = dot(weights, jnp.ones((ch, cols), BF16), 0, 0)
    row = [
        jnp.concatenate(
            [tmp[pl.ds(q * rows + i, share, stride=tiles * rows), :] for q in range(tiles)], 0
        ).astype(BF16)
        for i in range(rows)
    ]
    summed = dot(weights, jnp.concatenate(row, 1), 0, 0)
    return [
        (summed[:, i * cols : (i + 1) * cols] - columns * mean[i : i + 1]) * scale[i : i + 1]
        for i in range(rows)
    ]


def middle_kernel(p_ref, pair_ref, gate_ref, whole_ref, mid_ref, out_ref, tmp, tmp2):
    ch, rows, cols = p_ref.shape
    tiles = whole_ref.shape[0]
    share = ch // tiles
    updates = update_of(p_ref, whole_ref, 0, tmp)
    normed = []
    for i in range(rows):
        lanes = slice(i * cols, (i + 1) * cols)
        mid = (pair_ref[:, lanes].astype(F32) + gate_ref[:, lanes] * updates[i]).astype(BF16)
        mid_ref[:, lanes] = mid
        normed.append(norm_down(mid.astype(F32), None))
    weights = jnp.concatenate(
        [whole_ref[q, a * share : (a + 1) * share] for a in range(4) for q in range(tiles)], 0
    )
    parts = dot(weights, jnp.concatenate(normed, 1), 1, 0)
    for i in range(rows):
        lanes = slice(i * cols, (i + 1) * cols)
        for s in range(2):
            value = parts[2 * s * ch : (2 * s + 1) * ch, lanes]
            both = value + value * jnp.tanh(parts[(2 * s + 1) * ch : (2 * s + 2) * ch, lanes])
            for q in range(tiles):
                tmp2[s, pl.ds(q * rows + i, share, stride=tiles * rows), :] = both[q * share : (q + 1) * share]
    for s in range(2):
        out_ref[:, s] = tmp2[s].reshape(ch, rows, cols).astype(BF16)


def middle_step(p, pair, gate, whole):
    ch, rows, cols = p.shape
    return pl.pallas_call(
        middle_kernel,
        out_shape=(
            jax.ShapeDtypeStruct(pair.shape, BF16),
            jax.ShapeDtypeStruct((ch, 2, rows, cols), BF16),
        ),
        scratch_shapes=[pltpu.VMEM((ch * rows, cols), F32), pltpu.VMEM((2, ch * rows, cols), F32)],
        compiler_params=params(32),
        name="middle_step",
    )(p, pair, gate, whole)


def last_kernel(p_ref, mid_ref, gate_ref, whole_ref, out_ref, tmp):
    ch, rows, cols = p_ref.shape
    updates = update_of(p_ref, whole_ref, 1, tmp)
    for i in range(rows):
        lanes = slice(i * cols, (i + 1) * cols)
        out = mid_ref[:, lanes].astype(F32) + gate_ref[:, lanes] * updates[i]
        out_ref[i] = out.T.astype(BF16)


def last_step(p, mid, gate, whole):
    ch, rows, cols = p.shape
    return pl.pallas_call(
        last_kernel,
        out_shape=jax.ShapeDtypeStruct((rows, cols, mid.shape[0]), BF16),
        scratch_shapes=[pltpu.VMEM((ch * rows, cols), F32)],
        compiler_params=params(32),
        name="last_step",
    )(p, mid, gate, whole)


def on_device(pair_rep, proj_weight, gate_weight, out_weight, in_gain, out_gain):
    rows, width, ch = pair_rep.shape
    tiles = lax.axis_size("chan")
    blocks = lax.axis_size("blk")
    share = proj_weight.shape[3]
    cols = width // tiles
    everywhere = ("blk", "chan")

    turned = jnp.transpose(proj_weight, (0, 1, 3, 2))
    halves = project(pair_rep, turned, in_gain, cols)

    turned, out_weight, out_gain, gain, halves = lax.optimization_barrier(
        (turned, out_weight, out_gain, in_gain, halves)
    )
    later = (turned[1].astype(F32) * (0.5 * gain[1])).astype(BF16).reshape(4 * share, ch)
    scaled = (out_weight.astype(F32) * out_gain[:, :, None]).astype(BF16).reshape(2 * share, ch)
    packed = jnp.concatenate([later, scaled], 0)
    whole = lax.all_gather(packed, "chan", axis=0, tiled=False)
    own = lax.dynamic_slice_in_dim(pair_rep, lax.axis_index("chan") * cols, cols, 1)
    own, gate = first_gate(own, gate_weight, in_gain)

    halves = lax.all_to_all(halves, "blk", 0, 0, tiled=True)
    halves, whole, own, gate = lax.optimization_barrier((halves, whole, own, gate))
    product = outgoing(halves, tiles).reshape(blocks * tiles, rows, cols)
    product = lax.all_to_all(product, everywhere, 0, 0, tiled=True)
    mid, halves = middle_step(product, own, gate, whole)
    gate = second_gate(mid, gate_weight, in_gain)
    halves = lax.all_to_all(halves, everywhere, 0, 0, tiled=True)

    product = incoming(halves.reshape(blocks, tiles, 2, rows, cols)).reshape(blocks * tiles, rows, cols)
    product = lax.all_to_all(product, everywhere, 0, 0, tiled=True)
    return last_step(product, mid, gate, whole)


def solution(mesh):
    placed = (
        P("blk", None, None),
        P(None, None, None, "chan"),
        P(),
        P(None, "chan", None),
        P(),
        P(None, "chan"),
    )
    return jax.shard_map(
        on_device, mesh=mesh, in_specs=placed, out_specs=P("blk", "chan", None), check_vma=False
    )
```

```python
import jax
import jax.numpy as jnp
from jax import lax
from jax.experimental import pallas as pl
from jax.experimental.pallas import tpu as pltpu
from jax.sharding import PartitionSpec as P

epsilon = 1e-05
F32 = jnp.float32
BF16 = jnp.bfloat16
WHOLE = pl.BlockSpec(memory_space=pltpu.VMEM)


def params(mib):
    return pltpu.CompilerParams(vmem_limit_bytes=mib * 1024 * 1024)


def cost(flops, moved):
    return pl.CostEstimate(flops=flops, bytes_accessed=moved, transcendentals=0)


def dot(a, b, ca, cb):
    return lax.dot_general(a, b, (((ca,), (cb,)), ((), ())), preferred_element_type=F32)


def project_kernel(x_ref, w_ref, gain_ref, out_ref, tmp):
    rows, cols, ch = x_ref.shape
    share = out_ref.shape[0]
    weights = (w_ref[0].reshape(4 * share, ch).astype(F32) * gain_ref[0:1]).astype(BF16)
    x = jnp.concatenate([x_ref[i].T for i in range(rows)], 1).astype(F32)
    centered = x - jnp.sum(x, 0, keepdims=True) * (1.0 / ch)
    var = jnp.sum(centered * centered, 0, keepdims=True) * (1.0 / ch)
    scale = jnp.broadcast_to(0.5 * lax.rsqrt(var + epsilon), (share, rows * cols))
    parts = dot(weights, centered.astype(BF16), 1, 0)
    for i in range(rows):
        lanes = slice(i * cols, (i + 1) * cols)
        for s in range(2):
            value = parts[2 * s * share : (2 * s + 1) * share, lanes] * scale[:, lanes]
            gate = jnp.tanh(parts[(2 * s + 1) * share : (2 * s + 2) * share, lanes] * scale[:, lanes])
            tmp[s, pl.ds(i, share, stride=rows), :] = value + value * gate
    for s in range(2):
        out_ref[:, s] = tmp[s].reshape(share, rows, cols).astype(BF16)


def project(x, w, gain, cols):
    rows, width, ch = x.shape
    share = w.shape[2]
    return pl.pallas_call(
        project_kernel,
        grid=(width // cols,),
        in_specs=[pl.BlockSpec((rows, cols, ch), lambda t: (0, t, 0)), WHOLE, WHOLE],
        out_specs=pl.BlockSpec((share, 2, rows, cols), lambda t: (0, 0, 0, t)),
        out_shape=jax.ShapeDtypeStruct((share, 2, rows, width), BF16),
        scratch_shapes=[pltpu.VMEM((2, share * rows, cols), F32)],
        compiler_params=params(60),
        name="project_rows",
    )(x, w, gain)


def norm_down(x):
    ch = x.shape[0]
    centered = x - jnp.sum(x, 0, keepdims=True) * (1.0 / ch)
    var = jnp.sum(centered * centered, 0, keepdims=True) * (1.0 / ch)
    return (centered * lax.rsqrt(var + epsilon)).astype(BF16)


def gate_of(normed, w_ref, gain_ref, s):
    w = (w_ref[s].astype(F32).T * (0.5 * gain_ref[s : s + 1])).astype(BF16)
    return 0.5 + 0.5 * jnp.tanh(dot(w, normed, 1, 0))


def first_gate_kernel(x_ref, w_ref, gain_ref, turned_ref, gate_ref):
    rows, cols, ch = x_ref.shape
    turned = jnp.concatenate([x_ref[i].astype(F32).T for i in range(rows)], 1)
    turned_ref[...] = turned.astype(BF16)
    gate_ref[...] = gate_of(norm_down(turned), w_ref, gain_ref, 0)


def first_gate(x, w, gain):
    rows, cols, ch = x.shape
    return pl.pallas_call(
        first_gate_kernel,
        out_shape=(
            jax.ShapeDtypeStruct((ch, rows * cols), BF16),
            jax.ShapeDtypeStruct((ch, rows * cols), F32),
        ),
        compiler_params=params(32),
        cost_estimate=cost(2 * rows * cols * ch * ch, 8 * rows * cols * ch),
        name="first_gate",
    )(x, w, gain)


def outgoing_kernel(x_ref, out_ref):
    blocks, _, rows, n = x_ref.shape
    tiles, cols = out_ref.shape[1], out_ref.shape[3]
    left = x_ref[:, 0].reshape(blocks * rows, n)
    per = cols // rows
    for q in range(tiles):
        right = x_ref[q * per : (q + 1) * per, 1].reshape(cols, n)
        out_ref[:, q] = dot(left, right, 1, 1).reshape(blocks, rows, cols).astype(BF16)


def outgoing(x, tiles):
    blocks, _, rows, n = x.shape
    return pl.pallas_call(
        outgoing_kernel,
        out_shape=jax.ShapeDtypeStruct((blocks, tiles, rows, n // tiles), BF16),
        compiler_params=params(32),
        name="outgoing_product",
    )(x)


def incoming_kernel(x_ref, out_ref):
    blocks, tiles, _, rows, cols = x_ref.shape
    per = cols // rows
    rights = [x_ref[:, q, 1].reshape(blocks * rows, cols) for q in range(tiles)]
    right = jnp.concatenate(rights, axis=1)
    for p in range(tiles):
        left = x_ref[:, p, 0].reshape(blocks * rows, cols)
        product = dot(left, right, 0, 0).astype(BF16)
        for q in range(tiles):
            out_ref[p * per : (p + 1) * per, q] = product[:, q * cols : (q + 1) * cols].reshape(per, rows, cols)


def incoming(x):
    blocks, tiles, _, rows, cols = x.shape
    return pl.pallas_call(
        incoming_kernel,
        out_shape=jax.ShapeDtypeStruct((blocks, tiles, rows, cols), BF16),
        compiler_params=params(32),
        name="incoming_product",
    )(x)


def update_of(p_ref, whole_ref, s, tmp):
    ch, rows, cols = p_ref.shape
    tiles = whole_ref.shape[0]
    share = ch // tiles
    p = p_ref[...].astype(F32)
    tmp[...] = p.reshape(ch * rows, cols)
    mean = jnp.sum(p, 0) * (1.0 / ch)
    square = jnp.sum(p * p, 0) * (1.0 / ch)
    scale = lax.rsqrt(square - mean * mean + epsilon)
    weights = jnp.concatenate(
        [whole_ref[q, (4 + s) * share : (5 + s) * share] for q in range(tiles)], 0
    )
    columns = dot(weights, jnp.ones((ch, cols), BF16), 0, 0)
    row = [
        jnp.concatenate(
            [tmp[pl.ds(q * rows + i, share, stride=tiles * rows), :] for q in range(tiles)], 0
        ).astype(BF16)
        for i in range(rows)
    ]
    summed = dot(weights, jnp.concatenate(row, 1), 0, 0)
    return [
        (summed[:, i * cols : (i + 1) * cols] - columns * mean[i : i + 1]) * scale[i : i + 1]
        for i in range(rows)
    ]


def middle_kernel(p_ref, pair_ref, gate_ref, whole_ref, gw_ref, gain_ref, mid_ref, gate2_ref, out_ref, tmp, tmp2):
    ch, rows, cols = p_ref.shape
    tiles = whole_ref.shape[0]
    share = ch // tiles
    updates = update_of(p_ref, whole_ref, 0, tmp)
    normed = []
    for i in range(rows):
        lanes = slice(i * cols, (i + 1) * cols)
        mid = (pair_ref[:, lanes].astype(F32) + gate_ref[:, lanes] * updates[i]).astype(BF16)
        mid_ref[:, lanes] = mid
        normed.append(norm_down(mid.astype(F32)))
    weights = jnp.concatenate(
        [whole_ref[q, a * share : (a + 1) * share] for a in range(4) for q in range(tiles)], 0
    )
    normed = jnp.concatenate(normed, 1)
    parts = dot(weights, normed, 1, 0)
    for i in range(rows):
        lanes = slice(i * cols, (i + 1) * cols)
        for s in range(2):
            value = parts[2 * s * ch : (2 * s + 1) * ch, lanes]
            both = value + value * jnp.tanh(parts[(2 * s + 1) * ch : (2 * s + 2) * ch, lanes])
            for q in range(tiles):
                tmp2[s, pl.ds(q * rows + i, share, stride=tiles * rows), :] = both[q * share : (q + 1) * share]
    for s in range(2):
        out_ref[:, s] = tmp2[s].reshape(ch, rows, cols).astype(BF16)
    gate2_ref[...] = gate_of(normed, gw_ref, gain_ref, 1)


def middle_step(p, pair, gate, whole, gate_weight, in_gain):
    ch, rows, cols = p.shape
    return pl.pallas_call(
        middle_kernel,
        out_shape=(
            jax.ShapeDtypeStruct(pair.shape, BF16),
            jax.ShapeDtypeStruct(pair.shape, F32),
            jax.ShapeDtypeStruct((ch, 2, rows, cols), BF16),
        ),
        scratch_shapes=[pltpu.VMEM((ch * rows, cols), F32), pltpu.VMEM((2, ch * rows, cols), F32)],
        compiler_params=params(32),
        name="middle_step",
    )(p, pair, gate, whole, gate_weight, in_gain)


def last_kernel(p_ref, mid_ref, gate_ref, whole_ref, out_ref, tmp):
    ch, rows, cols = p_ref.shape
    updates = update_of(p_ref, whole_ref, 1, tmp)
    for i in range(rows):
        lanes = slice(i * cols, (i + 1) * cols)
        out = mid_ref[:, lanes].astype(F32) + gate_ref[:, lanes] * updates[i]
        out_ref[i] = out.T.astype(BF16)


def last_step(p, mid, gate, whole):
    ch, rows, cols = p.shape
    return pl.pallas_call(
        last_kernel,
        out_shape=jax.ShapeDtypeStruct((rows, cols, mid.shape[0]), BF16),
        scratch_shapes=[pltpu.VMEM((ch * rows, cols), F32)],
        compiler_params=params(32),
        name="last_step",
    )(p, mid, gate, whole)


def gather_small(x, axis):
    n = lax.axis_size(axis)
    me = lax.axis_index(axis)
    parts = [x] + [lax.ppermute(x, axis, [(i, i ^ k) for i in range(n)]) for k in range(1, n)]
    bit = 1
    while bit < n:
        swap = (me & bit) != 0
        parts = [jnp.where(swap, parts[k ^ bit], parts[k]) for k in range(n)]
        bit *= 2
    return jnp.stack(parts)


def on_device(pair_rep, proj_weight, gate_weight, out_weight, in_gain, out_gain):
    rows, width, ch = pair_rep.shape
    tiles = lax.axis_size("chan")
    blocks = lax.axis_size("blk")
    share = proj_weight.shape[3]
    cols = width // tiles
    everywhere = ("blk", "chan")

    turned = jnp.transpose(proj_weight, (0, 1, 3, 2))
    halves = project(pair_rep, turned, in_gain, cols)

    turned, out_weight, out_gain, gain, halves = lax.optimization_barrier(
        (turned, out_weight, out_gain, in_gain, halves)
    )
    later = (turned[1].astype(F32) * (0.5 * gain[1])).astype(BF16).reshape(4 * share, ch)
    scaled = (out_weight.astype(F32) * out_gain[:, :, None]).astype(BF16).reshape(2 * share, ch)
    packed = jnp.concatenate([later, scaled], 0)
    whole = gather_small(packed, "chan")
    own = lax.dynamic_slice_in_dim(pair_rep, lax.axis_index("chan") * cols, cols, 1)
    own, gate = first_gate(own, gate_weight, in_gain)

    halves = lax.all_to_all(halves, "blk", 0, 0, tiled=True)
    halves, whole, own, gate = lax.optimization_barrier((halves, whole, own, gate))
    product = outgoing(halves, tiles).reshape(blocks * tiles, rows, cols)
    product = lax.all_to_all(product, everywhere, 0, 0, tiled=True)
    mid, gate, halves = middle_step(product, own, gate, whole, gate_weight, in_gain)
    halves = lax.all_to_all(halves, everywhere, 0, 0, tiled=True)

    product = incoming(halves.reshape(blocks, tiles, 2, rows, cols)).reshape(blocks * tiles, rows, cols)
    product = lax.all_to_all(product, everywhere, 0, 0, tiled=True)
    return last_step(product, mid, gate, whole)


def solution(mesh):
    placed = (
        P("blk", None, None),
        P(None, None, None, "chan"),
        P(),
        P(None, "chan", None),
        P(),
        P(None, "chan"),
    )
    return jax.shard_map(
        on_device, mesh=mesh, in_specs=placed, out_specs=P("blk", "chan", None), check_vma=False
    )
```

```python
import jax
import jax.numpy as jnp
from jax import lax
from jax.experimental import pallas as pl
from jax.experimental.pallas import tpu as pltpu
from jax.sharding import PartitionSpec as P

epsilon = 1e-05
F32 = jnp.float32
BF16 = jnp.bfloat16
WHOLE = pl.BlockSpec(memory_space=pltpu.VMEM)


def params(mib):
    return pltpu.CompilerParams(vmem_limit_bytes=mib * 1024 * 1024)


def cost(flops, moved):
    return pl.CostEstimate(flops=flops, bytes_accessed=moved, transcendentals=0)


def dot(a, b, ca, cb):
    return lax.dot_general(a, b, (((ca,), (cb,)), ((), ())), preferred_element_type=F32)


def stacked(x, rows):
    cols = x.shape[1] // rows
    return jnp.swapaxes(jnp.stack([x[:, i * cols : (i + 1) * cols] for i in range(rows)], 0), 0, 1)


def project_kernel(x_ref, w_ref, gain_ref, out_ref):
    rows, cols, ch = x_ref.shape
    share = out_ref.shape[0]
    weights = (w_ref[0].reshape(4 * share, ch).astype(F32) * gain_ref[0:1]).astype(BF16)
    x = jnp.concatenate([x_ref[i].T for i in range(rows)], 1).astype(F32)
    centered = x - jnp.sum(x, 0, keepdims=True) * (1.0 / ch)
    var = jnp.sum(centered * centered, 0, keepdims=True) * (1.0 / ch)
    scale = jnp.broadcast_to(0.5 * lax.rsqrt(var + epsilon), (share, rows * cols))
    parts = dot(weights, centered.astype(BF16), 1, 0)
    for s in range(2):
        value = parts[2 * s * share : (2 * s + 1) * share] * scale
        gate = jnp.tanh(parts[(2 * s + 1) * share : (2 * s + 2) * share] * scale)
        out_ref[:, s] = stacked((value + value * gate).astype(BF16), rows)


def project(x, w, gain):
    rows, width, ch = x.shape
    share = w.shape[2]
    cols = width // 2
    return pl.pallas_call(
        project_kernel,
        grid=(width // cols,),
        in_specs=[pl.BlockSpec((rows, cols, ch), lambda t: (0, t, 0)), WHOLE, WHOLE],
        out_specs=pl.BlockSpec((share, 2, rows, cols), lambda t: (0, 0, 0, t)),
        out_shape=jax.ShapeDtypeStruct((share, 2, rows, width), BF16),
        compiler_params=params(60),
        name="project_rows",
    )(x, w, gain)


def norm_down(x):
    ch = x.shape[0]
    centered = x - jnp.sum(x, 0, keepdims=True) * (1.0 / ch)
    var = jnp.sum(centered * centered, 0, keepdims=True) * (1.0 / ch)
    return (centered * lax.rsqrt(var + epsilon)).astype(BF16)


def gate_of(normed, w_ref, gain_ref, s):
    w = (w_ref[s].astype(F32).T * (0.5 * gain_ref[s : s + 1])).astype(BF16)
    return 0.5 + 0.5 * jnp.tanh(dot(w, normed, 1, 0))


def first_gate_kernel(x_ref, w_ref, gain_ref, turned_ref, gate_ref):
    rows, cols, ch = x_ref.shape
    turned = jnp.concatenate([x_ref[i].astype(F32).T for i in range(rows)], 1)
    turned_ref[...] = turned.astype(BF16)
    gate_ref[...] = gate_of(norm_down(turned), w_ref, gain_ref, 0)


def first_gate(x, w, gain):
    rows, cols, ch = x.shape
    return pl.pallas_call(
        first_gate_kernel,
        out_shape=(
            jax.ShapeDtypeStruct((ch, rows * cols), BF16),
            jax.ShapeDtypeStruct((ch, rows * cols), F32),
        ),
        compiler_params=params(32),
        cost_estimate=cost(2 * rows * cols * ch * ch, 8 * rows * cols * ch),
        name="first_gate",
    )(x, w, gain)


def outgoing_kernel(x_ref, out_ref):
    blocks, _, rows, n = x_ref.shape
    tiles, cols = out_ref.shape[1], out_ref.shape[3]
    left = x_ref[:, 0].reshape(blocks * rows, n)
    per = cols // rows
    for q in range(tiles):
        right = x_ref[q * per : (q + 1) * per, 1].reshape(cols, n)
        out_ref[:, q] = dot(left, right, 1, 1).reshape(blocks, rows, cols).astype(BF16)


def outgoing(x, tiles):
    blocks, _, rows, n = x.shape
    return pl.pallas_call(
        outgoing_kernel,
        out_shape=jax.ShapeDtypeStruct((blocks, tiles, rows, n // tiles), BF16),
        compiler_params=params(32),
        name="outgoing_product",
    )(x)


def incoming_kernel(x_ref, out_ref):
    blocks, tiles, _, rows, cols = x_ref.shape
    per = cols // rows
    rights = [x_ref[:, q, 1].reshape(blocks * rows, cols) for q in range(tiles)]
    right = jnp.concatenate(rights, axis=1)
    for p in range(tiles):
        left = x_ref[:, p, 0].reshape(blocks * rows, cols)
        product = dot(left, right, 0, 0).astype(BF16)
        for q in range(tiles):
            out_ref[p * per : (p + 1) * per, q] = product[:, q * cols : (q + 1) * cols].reshape(per, rows, cols)


def incoming(x):
    blocks, tiles, _, rows, cols = x.shape
    return pl.pallas_call(
        incoming_kernel,
        out_shape=jax.ShapeDtypeStruct((blocks, tiles, rows, cols), BF16),
        compiler_params=params(32),
        name="incoming_product",
    )(x)


def update_of(p_ref, weights):
    ch, rows, cols = p_ref.shape
    p = p_ref[...].astype(F32)
    mean = jnp.sum(p, 0) * (1.0 / ch)
    square = jnp.sum(p * p, 0) * (1.0 / ch)
    scale = lax.rsqrt(square - mean * mean + epsilon)
    columns = dot(weights, jnp.ones((ch, cols), BF16), 0, 0)
    by_row = jnp.swapaxes(p_ref[...], 0, 1)
    summed = dot(weights, jnp.concatenate([by_row[i] for i in range(rows)], 1), 0, 0)
    return [
        (summed[:, i * cols : (i + 1) * cols] - columns * mean[i : i + 1]) * scale[i : i + 1]
        for i in range(rows)
    ]


def middle_kernel(p_ref, pair_ref, gate_ref, whole_ref, gw_ref, gain_ref, mid_ref, gate2_ref, out_ref):
    ch, rows, cols = p_ref.shape
    updates = update_of(p_ref, whole_ref[4])
    normed = []
    for i in range(rows):
        lanes = slice(i * cols, (i + 1) * cols)
        mid = (pair_ref[:, lanes].astype(F32) + gate_ref[:, lanes] * updates[i]).astype(BF16)
        mid_ref[:, lanes] = mid
        normed.append(norm_down(mid.astype(F32)))
    normed = jnp.concatenate(normed, 1)
    parts = dot(whole_ref[:4].reshape(4 * ch, ch), normed, 1, 0)
    for s in range(2):
        value = parts[2 * s * ch : (2 * s + 1) * ch]
        gate = jnp.tanh(parts[(2 * s + 1) * ch : (2 * s + 2) * ch])
        out_ref[:, s] = stacked((value + value * gate).astype(BF16), rows)
    gate2_ref[...] = gate_of(normed, gw_ref, gain_ref, 1)


def middle_step(p, pair, gate, whole, gate_weight, in_gain):
    ch, rows, cols = p.shape
    return pl.pallas_call(
        middle_kernel,
        out_shape=(
            jax.ShapeDtypeStruct(pair.shape, BF16),
            jax.ShapeDtypeStruct(pair.shape, F32),
            jax.ShapeDtypeStruct((ch, 2, rows, cols), BF16),
        ),
        compiler_params=params(32),
        name="middle_step",
    )(p, pair, gate, whole, gate_weight, in_gain)


def last_kernel(p_ref, mid_ref, gate_ref, whole_ref, out_ref):
    ch, rows, cols = p_ref.shape
    updates = update_of(p_ref, whole_ref[5])
    for i in range(rows):
        lanes = slice(i * cols, (i + 1) * cols)
        out = mid_ref[:, lanes].astype(F32) + gate_ref[:, lanes] * updates[i]
        out_ref[i] = out.astype(BF16).T


def last_step(p, mid, gate, whole):
    ch, rows, cols = p.shape
    return pl.pallas_call(
        last_kernel,
        out_shape=jax.ShapeDtypeStruct((rows, cols, mid.shape[0]), BF16),
        compiler_params=params(32),
        name="last_step",
    )(p, mid, gate, whole)


def gather_small(x, axis):
    n = lax.axis_size(axis)
    me = lax.axis_index(axis)
    parts = [x] + [lax.ppermute(x, axis, [(i, i ^ k) for i in range(n)]) for k in range(1, n)]
    bit = 1
    while bit < n:
        swap = (me & bit) != 0
        parts = [jnp.where(swap, parts[k ^ bit], parts[k]) for k in range(n)]
        bit *= 2
    return jnp.stack(parts, -2)


def on_device(pair_rep, proj_weight, gate_weight, out_weight, in_gain, out_gain):
    rows, width, ch = pair_rep.shape
    tiles = lax.axis_size("chan")
    blocks = lax.axis_size("blk")
    share = proj_weight.shape[3]
    cols = width // tiles
    everywhere = ("blk", "chan")

    turned = jnp.transpose(proj_weight, (0, 1, 3, 2))
    halves = project(pair_rep, turned, in_gain)

    turned, out_weight, out_gain, gain, halves = lax.optimization_barrier(
        (turned, out_weight, out_gain, in_gain, halves)
    )
    later = (turned[1].astype(F32) * (0.5 * gain[1])).astype(BF16)
    scaled = (out_weight.astype(F32) * out_gain[:, :, None]).astype(BF16)
    whole = gather_small(jnp.concatenate([later, scaled], 0), "chan")
    whole = whole.reshape(6, share * tiles, ch)
    own = lax.dynamic_slice_in_dim(pair_rep, lax.axis_index("chan") * cols, cols, 1)
    own, gate = first_gate(own, gate_weight, in_gain)

    halves = lax.all_to_all(halves, "blk", 0, 0, tiled=True)
    halves, whole, own, gate = lax.optimization_barrier((halves, whole, own, gate))
    product = outgoing(halves, tiles).reshape(blocks * tiles, rows, cols)
    product = lax.all_to_all(product, everywhere, 0, 0, tiled=True)
    mid, gate, halves = middle_step(product, own, gate, whole, gate_weight, in_gain)
    halves = lax.all_to_all(halves, everywhere, 0, 0, tiled=True)

    product = incoming(halves.reshape(blocks, tiles, 2, rows, cols)).reshape(blocks * tiles, rows, cols)
    product = lax.all_to_all(product, everywhere, 0, 0, tiled=True)
    return last_step(product, mid, gate, whole)


def solution(mesh):
    placed = (
        P("blk", None, None),
        P(None, None, None, "chan"),
        P(),
        P(None, "chan", None),
        P(),
        P(None, "chan"),
    )
    return jax.shard_map(
        on_device, mesh=mesh, in_specs=placed, out_specs=P("blk", "chan", None), check_vma=False
    )
```

```python
import jax
import jax.numpy as jnp
from jax import lax
from jax.experimental import pallas as pl
from jax.experimental.pallas import tpu as pltpu
from jax.sharding import PartitionSpec as P

epsilon = 1e-05
F32 = jnp.float32
BF16 = jnp.bfloat16
WHOLE = pl.BlockSpec(memory_space=pltpu.VMEM)


def params(mib):
    return pltpu.CompilerParams(vmem_limit_bytes=mib * 1024 * 1024)


def cost(flops, moved):
    return pl.CostEstimate(flops=flops, bytes_accessed=moved, transcendentals=0)


def dot(a, b, ca, cb):
    return lax.dot_general(a, b, (((ca,), (cb,)), ((), ())), preferred_element_type=F32)


def stacked(x, rows):
    cols = x.shape[1] // rows
    return jnp.swapaxes(jnp.stack([x[:, i * cols : (i + 1) * cols] for i in range(rows)], 0), 0, 1)


def project_kernel(x_ref, w_ref, gain_ref, out_ref):
    rows, cols, ch = x_ref.shape
    share = out_ref.shape[0]
    weights = (w_ref[0].reshape(4 * share, ch).astype(F32) * gain_ref[0:1]).astype(BF16)
    x = jnp.concatenate([x_ref[i].T for i in range(rows)], 1).astype(F32)
    centered = x - jnp.sum(x, 0, keepdims=True) * (1.0 / ch)
    var = jnp.sum(centered * centered, 0, keepdims=True) * (1.0 / ch)
    scale = jnp.broadcast_to(0.5 * lax.rsqrt(var + epsilon), (share, rows * cols))
    parts = dot(weights, centered.astype(BF16), 1, 0)
    for s in range(2):
        value = parts[2 * s * share : (2 * s + 1) * share] * scale
        gate = jnp.tanh(parts[(2 * s + 1) * share : (2 * s + 2) * share] * scale)
        out_ref[:, s] = stacked((value + value * gate).astype(BF16), rows)


def project(x, w, gain):
    rows, width, ch = x.shape
    share = w.shape[2]
    cols = width // 2
    return pl.pallas_call(
        project_kernel,
        grid=(width // cols,),
        in_specs=[pl.BlockSpec((rows, cols, ch), lambda t: (0, t, 0)), WHOLE, WHOLE],
        out_specs=pl.BlockSpec((share, 2, rows, cols), lambda t: (0, 0, 0, t)),
        out_shape=jax.ShapeDtypeStruct((share, 2, rows, width), BF16),
        compiler_params=params(60),
        name="project_rows",
    )(x, w, gain)


def norm_down(x):
    ch = x.shape[0]
    centered = x - jnp.sum(x, 0, keepdims=True) * (1.0 / ch)
    var = jnp.sum(centered * centered, 0, keepdims=True) * (1.0 / ch)
    return (centered * lax.rsqrt(var + epsilon)).astype(BF16)


def gate_of(normed, w_ref, gain_ref, s):
    w = (w_ref[s].astype(F32).T * (0.5 * gain_ref[s : s + 1])).astype(BF16)
    return 0.5 + 0.5 * jnp.tanh(dot(w, normed, 1, 0))


def first_gate_kernel(x_ref, w_ref, gain_ref, turned_ref, gate_ref):
    rows, cols, ch = x_ref.shape
    turned = jnp.concatenate([x_ref[i].astype(F32).T for i in range(rows)], 1)
    turned_ref[...] = turned.astype(BF16)
    gate_ref[...] = gate_of(norm_down(turned), w_ref, gain_ref, 0)


def first_gate(x, w, gain):
    rows, cols, ch = x.shape
    return pl.pallas_call(
        first_gate_kernel,
        out_shape=(
            jax.ShapeDtypeStruct((ch, rows * cols), BF16),
            jax.ShapeDtypeStruct((ch, rows * cols), F32),
        ),
        compiler_params=params(32),
        cost_estimate=cost(2 * rows * cols * ch * ch, 8 * rows * cols * ch),
        name="first_gate",
    )(x, w, gain)


def outgoing_kernel(x_ref, out_ref):
    blocks, _, rows, n = x_ref.shape
    tiles, cols = out_ref.shape[1], out_ref.shape[3]
    left = x_ref[:, 0].reshape(blocks * rows, n)
    per = cols // rows
    for q in range(tiles):
        right = x_ref[q * per : (q + 1) * per, 1].reshape(cols, n)
        out_ref[:, q] = dot(left, right, 1, 1).reshape(blocks, rows, cols).astype(BF16)


def outgoing(x, tiles):
    blocks, _, rows, n = x.shape
    return pl.pallas_call(
        outgoing_kernel,
        out_shape=jax.ShapeDtypeStruct((blocks, tiles, rows, n // tiles), BF16),
        compiler_params=params(32),
        name="outgoing_product",
    )(x)


def incoming_kernel(x_ref, out_ref):
    blocks, tiles, _, rows, cols = x_ref.shape
    per = cols // rows
    rights = [x_ref[:, q, 1].reshape(blocks * rows, cols) for q in range(tiles)]
    right = jnp.concatenate(rights, axis=1)
    for p in range(tiles):
        left = x_ref[:, p, 0].reshape(blocks * rows, cols)
        product = dot(left, right, 0, 0).astype(BF16)
        for q in range(tiles):
            out_ref[p * per : (p + 1) * per, q] = product[:, q * cols : (q + 1) * cols].reshape(per, rows, cols)


def incoming(x):
    blocks, tiles, _, rows, cols = x.shape
    return pl.pallas_call(
        incoming_kernel,
        out_shape=jax.ShapeDtypeStruct((blocks, tiles, rows, cols), BF16),
        compiler_params=params(32),
        name="incoming_product",
    )(x)


def update_of(p_ref, weights):
    ch, rows, cols = p_ref.shape
    p = p_ref[...].astype(F32)
    mean = jnp.sum(p, 0) * (1.0 / ch)
    square = jnp.sum(p * p, 0) * (1.0 / ch)
    scale = lax.rsqrt(square - mean * mean + epsilon)
    columns = dot(weights, jnp.ones((ch, cols), BF16), 0, 0)
    by_row = jnp.swapaxes(p_ref[...], 0, 1)
    summed = dot(weights, jnp.concatenate([by_row[i] for i in range(rows)], 1), 0, 0)
    return [
        (summed[:, i * cols : (i + 1) * cols] - columns * mean[i : i + 1]) * scale[i : i + 1]
        for i in range(rows)
    ]


def middle_kernel(p_ref, pair_ref, gate_ref, whole_ref, gw_ref, gain_ref, mid_ref, gate2_ref, out_ref):
    ch, rows, cols = p_ref.shape
    updates = update_of(p_ref, whole_ref[4])
    normed = []
    for i in range(rows):
        lanes = slice(i * cols, (i + 1) * cols)
        mid = (pair_ref[:, lanes].astype(F32) + gate_ref[:, lanes] * updates[i]).astype(BF16)
        mid_ref[:, lanes] = mid
        normed.append(norm_down(mid.astype(F32)))
    normed = jnp.concatenate(normed, 1)
    parts = dot(whole_ref[:4].reshape(4 * ch, ch), normed, 1, 0)
    for s in range(2):
        value = parts[2 * s * ch : (2 * s + 1) * ch]
        gate = jnp.tanh(parts[(2 * s + 1) * ch : (2 * s + 2) * ch])
        out_ref[:, s] = stacked((value + value * gate).astype(BF16), rows)
    gate2_ref[...] = gate_of(normed, gw_ref, gain_ref, 1)


def middle_step(p, pair, gate, whole, gate_weight, in_gain):
    ch, rows, cols = p.shape
    return pl.pallas_call(
        middle_kernel,
        out_shape=(
            jax.ShapeDtypeStruct(pair.shape, BF16),
            jax.ShapeDtypeStruct(pair.shape, F32),
            jax.ShapeDtypeStruct((ch, 2, rows, cols), BF16),
        ),
        compiler_params=params(32),
        name="middle_step",
    )(p, pair, gate, whole, gate_weight, in_gain)


def last_kernel(p_ref, mid_ref, gate_ref, whole_ref, out_ref):
    ch, rows, cols = p_ref.shape
    updates = update_of(p_ref, whole_ref[5])
    for i in range(rows):
        lanes = slice(i * cols, (i + 1) * cols)
        out = mid_ref[:, lanes].astype(F32) + gate_ref[:, lanes] * updates[i]
        out_ref[i] = out.astype(BF16).T


def last_step(p, mid, gate, whole):
    ch, rows, cols = p.shape
    return pl.pallas_call(
        last_kernel,
        out_shape=jax.ShapeDtypeStruct((rows, cols, mid.shape[0]), BF16),
        compiler_params=params(32),
        name="last_step",
    )(p, mid, gate, whole)


def gather_chan(x):
    n = lax.axis_size("chan")
    me = lax.axis_index("chan")
    far = n * lax.axis_size("blk") // 2
    parts = [x]
    for k in range(1, n):
        step = k ^ far if k & 2 else k
        pairs = [(i, i ^ step) for i in range(2 * far)]
        parts.append(lax.ppermute(x, ("blk", "chan"), pairs))
    bit = 1
    while bit < n:
        swap = (me & bit) != 0
        parts = [jnp.where(swap, parts[k ^ bit], parts[k]) for k in range(n)]
        bit *= 2
    return jnp.stack(parts, -2)


def on_device(pair_rep, proj_weight, gate_weight, out_weight, in_gain, out_gain):
    rows, width, ch = pair_rep.shape
    tiles = lax.axis_size("chan")
    blocks = lax.axis_size("blk")
    share = proj_weight.shape[3]
    cols = width // tiles
    everywhere = ("blk", "chan")

    turned = jnp.transpose(proj_weight, (0, 1, 3, 2))
    halves = project(pair_rep, turned, in_gain)

    turned, out_weight, out_gain, gain, halves = lax.optimization_barrier(
        (turned, out_weight, out_gain, in_gain, halves)
    )
    later = (turned[1].astype(F32) * (0.5 * gain[1])).astype(BF16)
    scaled = (out_weight.astype(F32) * out_gain[:, :, None]).astype(BF16)
    whole = gather_chan(jnp.concatenate([later, scaled], 0))
    whole = whole.reshape(6, share * tiles, ch)
    own = lax.dynamic_slice_in_dim(pair_rep, lax.axis_index("chan") * cols, cols, 1)
    own, gate = first_gate(own, gate_weight, in_gain)

    halves = lax.all_to_all(halves, "blk", 0, 0, tiled=True)
    halves, whole, own, gate = lax.optimization_barrier((halves, whole, own, gate))
    product = outgoing(halves, tiles).reshape(blocks * tiles, rows, cols)
    product = lax.all_to_all(product, everywhere, 0, 0, tiled=True)
    mid, gate, halves = middle_step(product, own, gate, whole, gate_weight, in_gain)
    halves = lax.all_to_all(halves, everywhere, 0, 0, tiled=True)

    product = incoming(halves.reshape(blocks, tiles, 2, rows, cols)).reshape(blocks * tiles, rows, cols)
    product = lax.all_to_all(product, everywhere, 0, 0, tiled=True)
    return last_step(product, mid, gate, whole)


def solution(mesh):
    placed = (
        P("blk", None, None),
        P(None, None, None, "chan"),
        P(),
        P(None, "chan", None),
        P(),
        P(None, "chan"),
    )
    return jax.shard_map(
        on_device, mesh=mesh, in_specs=placed, out_specs=P("blk", "chan", None), check_vma=False
    )
```

```python
import jax
import jax.numpy as jnp
from jax import lax
from jax.experimental import pallas as pl
from jax.experimental.pallas import tpu as pltpu
from jax.sharding import PartitionSpec as P

epsilon = 1e-05
F32 = jnp.float32
BF16 = jnp.bfloat16
WHOLE = pl.BlockSpec(memory_space=pltpu.VMEM)


def params(mib):
    return pltpu.CompilerParams(vmem_limit_bytes=mib * 1024 * 1024)


def cost(flops, moved):
    return pl.CostEstimate(flops=flops, bytes_accessed=moved, transcendentals=0)


def dot(a, b, ca, cb):
    return lax.dot_general(a, b, (((ca,), (cb,)), ((), ())), preferred_element_type=F32)


def center_down(x):
    ch = x.shape[0]
    eye = lax.broadcasted_iota(jnp.int32, (ch, ch), 0) == lax.broadcasted_iota(jnp.int32, (ch, ch), 1)
    center = (jnp.where(eye, 1.0, 0.0) - 1.0 / ch).astype(BF16)
    centered = dot(center, x, 1, 0)
    rounded = centered.astype(BF16)
    var = dot(jnp.full((16, ch), 1.0 / ch, BF16), rounded * rounded, 1, 0)[:8]
    return centered, var


def stacked(x, rows):
    cols = x.shape[1] // rows
    return jnp.swapaxes(jnp.stack([x[:, i * cols : (i + 1) * cols] for i in range(rows)], 0), 0, 1)


def project_kernel(x_ref, w_ref, gain_ref, out_ref):
    rows, cols, ch = x_ref.shape
    share = out_ref.shape[0]
    weights = (w_ref[0].reshape(4 * share, ch).astype(F32) * gain_ref[0:1]).astype(BF16)
    x = jnp.concatenate([x_ref[i].T for i in range(rows)], 1)
    centered, var = center_down(x)
    scale = 0.5 * lax.rsqrt(var + epsilon)
    scale = jnp.concatenate([scale] * (share // scale.shape[0]), 0)
    parts = dot(weights, centered.astype(BF16), 1, 0)
    for s in range(2):
        value = parts[2 * s * share : (2 * s + 1) * share] * scale
        gate = jnp.tanh(parts[(2 * s + 1) * share : (2 * s + 2) * share] * scale)
        out_ref[:, s] = stacked((value + value * gate).astype(BF16), rows)


def project(x, w, gain):
    rows, width, ch = x.shape
    share = w.shape[2]
    cols = width // 2
    return pl.pallas_call(
        project_kernel,
        grid=(width // cols,),
        in_specs=[pl.BlockSpec((rows, cols, ch), lambda t: (0, t, 0)), WHOLE, WHOLE],
        out_specs=pl.BlockSpec((share, 2, rows, cols), lambda t: (0, 0, 0, t)),
        out_shape=jax.ShapeDtypeStruct((share, 2, rows, width), BF16),
        compiler_params=params(60),
        name="project_rows",
    )(x, w, gain)


def norm_down(x):
    centered, var = center_down(x)
    return (centered * lax.rsqrt(var[:1] + epsilon)).astype(BF16)


def gate_of(normed, w_ref, gain_ref, s):
    w = (w_ref[s].astype(F32).T * (0.5 * gain_ref[s : s + 1])).astype(BF16)
    return 0.5 + 0.5 * jnp.tanh(dot(w, normed, 1, 0))


def first_gate_kernel(x_ref, w_ref, gain_ref, turned_ref, gate_ref):
    rows, cols, ch = x_ref.shape
    turned = jnp.concatenate([x_ref[i].T for i in range(rows)], 1)
    turned_ref[...] = turned
    gate_ref[...] = gate_of(norm_down(turned), w_ref, gain_ref, 0)


def first_gate(x, w, gain):
    rows, cols, ch = x.shape
    return pl.pallas_call(
        first_gate_kernel,
        out_shape=(
            jax.ShapeDtypeStruct((ch, rows * cols), BF16),
            jax.ShapeDtypeStruct((ch, rows * cols), F32),
        ),
        compiler_params=params(32),
        cost_estimate=cost(2 * rows * cols * ch * ch, 8 * rows * cols * ch),
        name="first_gate",
    )(x, w, gain)


def outgoing_kernel(x_ref, out_ref):
    blocks, _, rows, n = x_ref.shape
    tiles, cols = out_ref.shape[1], out_ref.shape[3]
    left = x_ref[:, 0].reshape(blocks * rows, n)
    right = x_ref[:, 1].reshape(blocks * rows, n)
    product = dot(left, right, 1, 1).astype(BF16)
    for q in range(tiles):
        out_ref[:, q] = product[:, q * cols : (q + 1) * cols].reshape(blocks, rows, cols)


def outgoing(x, tiles):
    blocks, _, rows, n = x.shape
    return pl.pallas_call(
        outgoing_kernel,
        out_shape=jax.ShapeDtypeStruct((blocks, tiles, rows, n // tiles), BF16),
        compiler_params=params(32),
        name="outgoing_product",
    )(x)


def incoming_kernel(x_ref, out_ref):
    blocks, tiles, _, rows, cols = x_ref.shape
    per = cols // rows
    rights = [x_ref[:, q, 1].reshape(blocks * rows, cols) for q in range(tiles)]
    right = jnp.concatenate(rights, axis=1)
    for p in range(tiles):
        left = x_ref[:, p, 0].reshape(blocks * rows, cols)
        product = dot(left, right, 0, 0).astype(BF16)
        for q in range(tiles):
            out_ref[p * per : (p + 1) * per, q] = product[:, q * cols : (q + 1) * cols].reshape(per, rows, cols)


def incoming(x):
    blocks, tiles, _, rows, cols = x.shape
    return pl.pallas_call(
        incoming_kernel,
        out_shape=jax.ShapeDtypeStruct((blocks, tiles, rows, cols), BF16),
        compiler_params=params(32),
        name="incoming_product",
    )(x)


def update_of(p_ref, weights):
    ch, rows, cols = p_ref.shape
    p = p_ref[...].astype(F32)
    mean = jnp.sum(p, 0) * (1.0 / ch)
    square = jnp.sum(p * p, 0) * (1.0 / ch)
    scale = lax.rsqrt(jnp.maximum(square - mean * mean, 0.0) + epsilon)
    columns = dot(weights, jnp.ones((ch, cols), BF16), 0, 0)
    by_row = jnp.swapaxes(p_ref[...], 0, 1)
    summed = dot(weights, jnp.concatenate([by_row[i] for i in range(rows)], 1), 0, 0)
    return [
        (summed[:, i * cols : (i + 1) * cols] - columns * mean[i : i + 1]) * scale[i : i + 1]
        for i in range(rows)
    ]


def middle_kernel(p_ref, pair_ref, gate_ref, whole_ref, gw_ref, gain_ref, mid_ref, gate2_ref, out_ref):
    ch, rows, cols = p_ref.shape
    updates = update_of(p_ref, whole_ref[4])
    mids = []
    for i in range(rows):
        lanes = slice(i * cols, (i + 1) * cols)
        mid = (pair_ref[:, lanes].astype(F32) + gate_ref[:, lanes] * updates[i]).astype(BF16)
        mid_ref[:, lanes] = mid
        mids.append(mid)
    normed = norm_down(jnp.concatenate(mids, 1))
    parts = dot(whole_ref[:4].reshape(4 * ch, ch), normed, 1, 0)
    for s in range(2):
        value = parts[2 * s * ch : (2 * s + 1) * ch]
        gate = jnp.tanh(parts[(2 * s + 1) * ch : (2 * s + 2) * ch])
        out_ref[:, s] = stacked((value + value * gate).astype(BF16), rows)
    gate2_ref[...] = gate_of(normed, gw_ref, gain_ref, 1)


def middle_step(p, pair, gate, whole, gate_weight, in_gain):
    ch, rows, cols = p.shape
    return pl.pallas_call(
        middle_kernel,
        out_shape=(
            jax.ShapeDtypeStruct(pair.shape, BF16),
            jax.ShapeDtypeStruct(pair.shape, F32),
            jax.ShapeDtypeStruct((ch, 2, rows, cols), BF16),
        ),
        compiler_params=params(32),
        name="middle_step",
    )(p, pair, gate, whole, gate_weight, in_gain)


def last_kernel(p_ref, mid_ref, gate_ref, whole_ref, out_ref):
    ch, rows, cols = p_ref.shape
    updates = update_of(p_ref, whole_ref[5])
    for i in range(rows):
        lanes = slice(i * cols, (i + 1) * cols)
        out = mid_ref[:, lanes].astype(F32) + gate_ref[:, lanes] * updates[i]
        out_ref[i] = out.astype(BF16).T


def last_step(p, mid, gate, whole):
    ch, rows, cols = p.shape
    return pl.pallas_call(
        last_kernel,
        out_shape=jax.ShapeDtypeStruct((rows, cols, mid.shape[0]), BF16),
        compiler_params=params(32),
        name="last_step",
    )(p, mid, gate, whole)


def gather_chan(x):
    n = lax.axis_size("chan")
    me = lax.axis_index("chan")
    far = n * lax.axis_size("blk") // 2
    parts = [x]
    for k in range(1, n):
        step = k ^ far if k & 2 else k
        pairs = [(i, i ^ step) for i in range(2 * far)]
        parts.append(lax.ppermute(x, ("blk", "chan"), pairs))
    bit = 1
    while bit < n:
        swap = (me & bit) != 0
        parts = [jnp.where(swap, parts[k ^ bit], parts[k]) for k in range(n)]
        bit *= 2
    return jnp.stack(parts, -2)


def on_device(pair_rep, proj_weight, gate_weight, out_weight, in_gain, out_gain):
    rows, width, ch = pair_rep.shape
    tiles = lax.axis_size("chan")
    blocks = lax.axis_size("blk")
    share = proj_weight.shape[3]
    cols = width // tiles
    everywhere = ("blk", "chan")

    turned = jnp.transpose(proj_weight, (0, 1, 3, 2))
    halves = project(pair_rep, turned, in_gain)

    turned, out_weight, out_gain, gain, halves = lax.optimization_barrier(
        (turned, out_weight, out_gain, in_gain, halves)
    )
    later = (turned[1].astype(F32) * (0.5 * gain[1])).astype(BF16)
    scaled = (out_weight.astype(F32) * out_gain[:, :, None]).astype(BF16)
    whole = gather_chan(jnp.concatenate([later, scaled], 0))
    whole = whole.reshape(6, share * tiles, ch)
    own = lax.dynamic_slice_in_dim(pair_rep, lax.axis_index("chan") * cols, cols, 1)
    own, gate = first_gate(own, gate_weight, in_gain)

    halves = lax.all_to_all(halves, "blk", 0, 0, tiled=True)
    halves, whole, own, gate = lax.optimization_barrier((halves, whole, own, gate))
    product = outgoing(halves, tiles).reshape(blocks * tiles, rows, cols)
    product = lax.all_to_all(product, everywhere, 0, 0, tiled=True)
    mid, gate, halves = middle_step(product, own, gate, whole, gate_weight, in_gain)
    halves = lax.all_to_all(halves, everywhere, 0, 0, tiled=True)

    product = incoming(halves.reshape(blocks, tiles, 2, rows, cols)).reshape(blocks * tiles, rows, cols)
    product = lax.all_to_all(product, everywhere, 0, 0, tiled=True)
    return last_step(product, mid, gate, whole)


def solution(mesh):
    placed = (
        P("blk", None, None),
        P(None, None, None, "chan"),
        P(),
        P(None, "chan", None),
        P(),
        P(None, "chan"),
    )
    return jax.shard_map(
        on_device, mesh=mesh, in_specs=placed, out_specs=P("blk", "chan", None), check_vma=False
    )
```

```python
import jax
import jax.numpy as jnp
from jax import lax
from jax.experimental import pallas as pl
from jax.experimental.pallas import tpu as pltpu
from jax.sharding import PartitionSpec as P

epsilon = 1e-05
F32 = jnp.float32
BF16 = jnp.bfloat16
WHOLE = pl.BlockSpec(memory_space=pltpu.VMEM)


def params(mib):
    return pltpu.CompilerParams(vmem_limit_bytes=mib * 1024 * 1024)


def cost(flops, moved):
    return pl.CostEstimate(flops=flops, bytes_accessed=moved, transcendentals=0)


def dot(a, b, ca, cb):
    return lax.dot_general(a, b, (((ca,), (cb,)), ((), ())), preferred_element_type=F32)


def center_down(x):
    ch = x.shape[0]
    eye = lax.broadcasted_iota(jnp.int32, (ch, ch), 0) == lax.broadcasted_iota(jnp.int32, (ch, ch), 1)
    center = (jnp.where(eye, 1.0, 0.0) - 1.0 / ch).astype(BF16)
    centered = dot(center, x, 1, 0)
    rounded = centered.astype(BF16)
    var = dot(jnp.full((16, ch), 1.0 / ch, BF16), rounded * rounded, 1, 0)[:8]
    return centered, var


def stacked(x, rows):
    cols = x.shape[1] // rows
    return jnp.swapaxes(jnp.stack([x[:, i * cols : (i + 1) * cols] for i in range(rows)], 0), 0, 1)


def project_kernel(x_ref, w_ref, gain_ref, out_ref):
    rows, cols, ch = x_ref.shape
    share = out_ref.shape[0]
    weights = (w_ref[0].reshape(4 * share, ch).astype(F32) * gain_ref[0:1]).astype(BF16)
    x = jnp.concatenate([x_ref[i].T for i in range(rows)], 1)
    centered, var = center_down(x)
    scale = 0.5 * lax.rsqrt(var + epsilon)
    scale = jnp.concatenate([scale] * (share // scale.shape[0]), 0)
    parts = dot(weights, centered.astype(BF16), 1, 0)
    for s in range(2):
        value = parts[2 * s * share : (2 * s + 1) * share] * scale
        gate = jnp.tanh(parts[(2 * s + 1) * share : (2 * s + 2) * share] * scale)
        out_ref[:, s] = stacked((value + value * gate).astype(BF16), rows)


def project(x, w, gain):
    rows, width, ch = x.shape
    share = w.shape[2]
    cols = width // 2
    return pl.pallas_call(
        project_kernel,
        grid=(width // cols,),
        in_specs=[pl.BlockSpec((rows, cols, ch), lambda t: (0, t, 0)), WHOLE, WHOLE],
        out_specs=pl.BlockSpec((share, 2, rows, cols), lambda t: (0, 0, 0, t)),
        out_shape=jax.ShapeDtypeStruct((share, 2, rows, width), BF16),
        compiler_params=params(60),
        name="project_rows",
    )(x, w, gain)


def norm_down(x):
    centered, var = center_down(x)
    return (centered * lax.rsqrt(var[:1] + epsilon)).astype(BF16)


def gate_of(normed, w_ref, gain_ref, s):
    w = (w_ref[s].astype(F32).T * (0.5 * gain_ref[s : s + 1])).astype(BF16)
    return 0.5 + 0.5 * jnp.tanh(dot(w, normed, 1, 0))


def first_gate_kernel(x_ref, w_ref, gain_ref, turned_ref, gate_ref):
    rows, cols, ch = x_ref.shape
    turned = jnp.concatenate([x_ref[i].T for i in range(rows)], 1)
    turned_ref[...] = turned
    gate_ref[...] = gate_of(norm_down(turned), w_ref, gain_ref, 0)


def first_gate(x, w, gain):
    rows, cols, ch = x.shape
    return pl.pallas_call(
        first_gate_kernel,
        out_shape=(
            jax.ShapeDtypeStruct((ch, rows * cols), BF16),
            jax.ShapeDtypeStruct((ch, rows * cols), F32),
        ),
        compiler_params=params(32),
        cost_estimate=cost(2 * rows * cols * ch * ch, 8 * rows * cols * ch),
        name="first_gate",
    )(x, w, gain)


def outgoing_kernel(x_ref, out_ref):
    blocks, _, rows, n = x_ref.shape
    tiles, cols = out_ref.shape[1], out_ref.shape[3]
    left = x_ref[:, 0].reshape(blocks * rows, n)
    right = x_ref[:, 1].reshape(blocks * rows, n)
    product = dot(left, right, 1, 1).astype(BF16)
    for q in range(tiles):
        out_ref[:, q] = product[:, q * cols : (q + 1) * cols].reshape(blocks, rows, cols)


def outgoing(x, tiles):
    blocks, _, rows, n = x.shape
    return pl.pallas_call(
        outgoing_kernel,
        out_shape=jax.ShapeDtypeStruct((blocks, tiles, rows, n // tiles), BF16),
        compiler_params=params(32),
        name="outgoing_product",
    )(x)


def incoming_kernel(x_ref, out_ref):
    blocks, tiles, _, rows, cols = x_ref.shape
    per = cols // rows
    rights = [x_ref[:, q, 1].reshape(blocks * rows, cols) for q in range(tiles)]
    right = jnp.concatenate(rights, axis=1)
    for p in range(tiles):
        left = x_ref[:, p, 0].reshape(blocks * rows, cols)
        product = dot(left, right, 0, 0).astype(BF16)
        for q in range(tiles):
            out_ref[p * per : (p + 1) * per, q] = product[:, q * cols : (q + 1) * cols].reshape(per, rows, cols)


def incoming(x):
    blocks, tiles, _, rows, cols = x.shape
    return pl.pallas_call(
        incoming_kernel,
        out_shape=jax.ShapeDtypeStruct((blocks, tiles, rows, cols), BF16),
        compiler_params=params(32),
        name="incoming_product",
    )(x)


def update_of(p_ref, weights):
    ch, rows, cols = p_ref.shape
    p = p_ref[...].astype(F32)
    mean = jnp.sum(p, 0) * (1.0 / ch)
    square = jnp.sum(p * p, 0) * (1.0 / ch)
    scale = lax.rsqrt(jnp.maximum(square - mean * mean, 0.0) + epsilon)
    columns = dot(weights, jnp.ones((ch, cols), BF16), 0, 0)
    by_row = jnp.swapaxes(p_ref[...], 0, 1)
    summed = dot(weights, jnp.concatenate([by_row[i] for i in range(rows)], 1), 0, 0)
    return [
        (summed[:, i * cols : (i + 1) * cols] - columns * mean[i : i + 1]) * scale[i : i + 1]
        for i in range(rows)
    ]


def middle_kernel(p_ref, pair_ref, gate_ref, whole_ref, gw_ref, gain_ref, mid_ref, gate2_ref, out_ref):
    ch, rows, cols = p_ref.shape
    updates = update_of(p_ref, whole_ref[4])
    mids = []
    for i in range(rows):
        lanes = slice(i * cols, (i + 1) * cols)
        mid = (pair_ref[:, lanes].astype(F32) + gate_ref[:, lanes] * updates[i]).astype(BF16)
        mid_ref[:, lanes] = mid
        mids.append(mid)
    mid = jnp.concatenate(mids, 1).astype(F32)
    centered = mid - jnp.sum(mid, 0, keepdims=True) * (1.0 / ch)
    var = jnp.sum(centered * centered, 0, keepdims=True) * (1.0 / ch)
    normed = (centered * lax.rsqrt(var + epsilon)).astype(BF16)
    parts = dot(whole_ref[:4].reshape(4 * ch, ch), normed, 1, 0)
    for s in range(2):
        value = parts[2 * s * ch : (2 * s + 1) * ch]
        gate = jnp.tanh(parts[(2 * s + 1) * ch : (2 * s + 2) * ch])
        out_ref[:, s] = stacked((value + value * gate).astype(BF16), rows)
    gate2_ref[...] = gate_of(normed, gw_ref, gain_ref, 1)


def middle_step(p, pair, gate, whole, gate_weight, in_gain):
    ch, rows, cols = p.shape
    return pl.pallas_call(
        middle_kernel,
        out_shape=(
            jax.ShapeDtypeStruct(pair.shape, BF16),
            jax.ShapeDtypeStruct(pair.shape, F32),
            jax.ShapeDtypeStruct((ch, 2, rows, cols), BF16),
        ),
        compiler_params=params(32),
        name="middle_step",
    )(p, pair, gate, whole, gate_weight, in_gain)


def last_kernel(p_ref, mid_ref, gate_ref, whole_ref, out_hbm, buffer, sem):
    ch, rows, cols = p_ref.shape
    parts = sem.shape[0]
    per = rows // parts
    updates = update_of(p_ref, whole_ref[5])
    copies = []
    for g in range(parts):
        group = slice(g * per, (g + 1) * per)
        for i in range(g * per, (g + 1) * per):
            lanes = slice(i * cols, (i + 1) * cols)
            out = mid_ref[:, lanes].astype(F32) + gate_ref[:, lanes] * updates[i]
            buffer[i] = out.astype(BF16).T
        copies.append(pltpu.make_async_copy(buffer.at[group], out_hbm.at[group], sem.at[g]))
        copies[-1].start()
    for copy in copies:
        copy.wait()


def last_step(p, mid, gate, whole):
    ch, rows, cols = p.shape
    out = (rows, cols, mid.shape[0])
    return pl.pallas_call(
        last_kernel,
        in_specs=[WHOLE] * 4,
        out_specs=pl.BlockSpec(memory_space=pl.ANY),
        out_shape=jax.ShapeDtypeStruct(out, BF16),
        scratch_shapes=[pltpu.VMEM(out, BF16), pltpu.SemaphoreType.DMA((4,))],
        compiler_params=params(32),
        name="last_step",
    )(p, mid, gate, whole)


def gather_chan(x):
    n = lax.axis_size("chan")
    me = lax.axis_index("chan")
    far = n * lax.axis_size("blk") // 2
    parts = [x]
    for k in range(1, n):
        step = k ^ far if k & 2 else k
        pairs = [(i, i ^ step) for i in range(2 * far)]
        parts.append(lax.ppermute(x, ("blk", "chan"), pairs))
    bit = 1
    while bit < n:
        swap = (me & bit) != 0
        parts = [jnp.where(swap, parts[k ^ bit], parts[k]) for k in range(n)]
        bit *= 2
    return jnp.stack(parts, -2)


def on_device(pair_rep, proj_weight, gate_weight, out_weight, in_gain, out_gain):
    rows, width, ch = pair_rep.shape
    tiles = lax.axis_size("chan")
    blocks = lax.axis_size("blk")
    share = proj_weight.shape[3]
    cols = width // tiles
    everywhere = ("blk", "chan")

    turned = jnp.transpose(proj_weight, (0, 1, 3, 2))
    halves = project(pair_rep, turned, in_gain)

    turned, out_weight, out_gain, gain, halves = lax.optimization_barrier(
        (turned, out_weight, out_gain, in_gain, halves)
    )
    later = (turned[1].astype(F32) * (0.5 * gain[1])).astype(BF16)
    scaled = (out_weight.astype(F32) * out_gain[:, :, None]).astype(BF16)
    whole = gather_chan(jnp.concatenate([later, scaled], 0))
    whole = whole.reshape(6, share * tiles, ch)
    own = lax.dynamic_slice_in_dim(pair_rep, lax.axis_index("chan") * cols, cols, 1)
    own, gate = first_gate(own, gate_weight, in_gain)

    halves = lax.all_to_all(halves, "blk", 0, 0, tiled=True)
    halves, whole, own, gate = lax.optimization_barrier((halves, whole, own, gate))
    product = outgoing(halves, tiles).reshape(blocks * tiles, rows, cols)
    product = lax.all_to_all(product, everywhere, 0, 0, tiled=True)
    mid, gate, halves = middle_step(product, own, gate, whole, gate_weight, in_gain)
    halves = lax.all_to_all(halves, everywhere, 0, 0, tiled=True)

    product = incoming(halves.reshape(blocks, tiles, 2, rows, cols)).reshape(blocks * tiles, rows, cols)
    product = lax.all_to_all(product, everywhere, 0, 0, tiled=True)
    return last_step(product, mid, gate, whole)


def solution(mesh):
    placed = (
        P("blk", None, None),
        P(None, None, None, "chan"),
        P(),
        P(None, "chan", None),
        P(),
        P(None, "chan"),
    )
    return jax.shard_map(
        on_device, mesh=mesh, in_specs=placed, out_specs=P("blk", "chan", None), check_vma=False
    )
```

```python
import jax
import jax.numpy as jnp
from jax import lax
from jax.experimental import pallas as pl
from jax.experimental.pallas import tpu as pltpu
from jax.sharding import PartitionSpec as P

epsilon = 1e-05
F32 = jnp.float32
BF16 = jnp.bfloat16
WHOLE = pl.BlockSpec(memory_space=pltpu.VMEM)


def params(mib):
    return pltpu.CompilerParams(vmem_limit_bytes=mib * 1024 * 1024)


def cost(flops, moved):
    return pl.CostEstimate(flops=flops, bytes_accessed=moved, transcendentals=0)


def dot(a, b, ca, cb):
    return lax.dot_general(a, b, (((ca,), (cb,)), ((), ())), preferred_element_type=F32)


def center_down(x):
    ch = x.shape[0]
    eye = lax.broadcasted_iota(jnp.int32, (ch, ch), 0) == lax.broadcasted_iota(jnp.int32, (ch, ch), 1)
    center = (jnp.where(eye, 1.0, 0.0) - 1.0 / ch).astype(BF16)
    centered = dot(center, x, 1, 0)
    rounded = centered.astype(BF16)
    var = dot(jnp.full((16, ch), 1.0 / ch, BF16), rounded * rounded, 1, 0)[:8]
    return centered, var


def stacked(x, rows):
    cols = x.shape[1] // rows
    return jnp.swapaxes(jnp.stack([x[:, i * cols : (i + 1) * cols] for i in range(rows)], 0), 0, 1)


def project_kernel(x_ref, w_ref, gain_ref, out_ref):
    rows, cols, ch = x_ref.shape
    share = out_ref.shape[0]
    weights = (w_ref[0].reshape(4 * share, ch).astype(F32) * gain_ref[0:1]).astype(BF16)
    centered, var = center_down(x_ref[...].reshape(rows * cols, ch).T)
    centered = centered.astype(BF16)
    scale = 0.5 * lax.rsqrt(var + epsilon)
    scale = jnp.concatenate([scale] * (share // scale.shape[0]), 0)
    for s in range(2):
        parts = dot(weights[2 * s * share : (2 * s + 2) * share], centered, 1, 0)
        value = parts[:share] * scale
        gate = jnp.tanh(parts[share:] * scale)
        out_ref[:, s] = stacked((value + value * gate).astype(BF16), rows)


def project(x, w, gain):
    rows, width, ch = x.shape
    share = w.shape[2]
    cols = width // 2
    return pl.pallas_call(
        project_kernel,
        grid=(width // cols,),
        in_specs=[
            pl.BlockSpec((rows, cols, ch), lambda t: (0, t, 0)),
            pl.BlockSpec((1, *w.shape[1:]), lambda t: (0, 0, 0, 0)),
            WHOLE,
        ],
        out_specs=pl.BlockSpec((share, 2, rows, cols), lambda t: (0, 0, 0, t)),
        out_shape=jax.ShapeDtypeStruct((share, 2, rows, width), BF16),
        compiler_params=params(60),
        name="project_rows",
    )(x, w, gain)


def norm_down(x):
    centered, var = center_down(x)
    return (centered * lax.rsqrt(var[:1] + epsilon)).astype(BF16)


def gate_of(normed, w_ref, gain_ref, s):
    w = (w_ref[s].astype(F32).T * (0.5 * gain_ref[s : s + 1])).astype(BF16)
    return 0.5 + 0.5 * jnp.tanh(dot(w, normed, 1, 0))


def first_gate_kernel(x_ref, w_ref, gain_ref, turned_ref, gate_ref):
    rows, cols, ch = x_ref.shape
    turned = jnp.concatenate([x_ref[i].T for i in range(rows)], 1)
    turned_ref[...] = turned
    gate_ref[...] = gate_of(norm_down(turned), w_ref, gain_ref, 0)


def first_gate(x, w, gain):
    rows, cols, ch = x.shape
    return pl.pallas_call(
        first_gate_kernel,
        out_shape=(
            jax.ShapeDtypeStruct((ch, rows * cols), BF16),
            jax.ShapeDtypeStruct((ch, rows * cols), F32),
        ),
        compiler_params=params(32),
        cost_estimate=cost(2 * rows * cols * ch * ch, 8 * rows * cols * ch),
        name="first_gate",
    )(x, w, gain)


def outgoing_kernel(x_ref, out_ref):
    blocks, _, rows, n = x_ref.shape
    tiles, cols = out_ref.shape[1], out_ref.shape[3]
    left = x_ref[:, 0].reshape(blocks * rows, n)
    right = x_ref[:, 1].reshape(blocks * rows, n)
    product = dot(left, right, 1, 1).astype(BF16)
    for q in range(tiles):
        out_ref[:, q] = product[:, q * cols : (q + 1) * cols].reshape(blocks, rows, cols)


def outgoing(x, tiles):
    blocks, _, rows, n = x.shape
    return pl.pallas_call(
        outgoing_kernel,
        out_shape=jax.ShapeDtypeStruct((blocks, tiles, rows, n // tiles), BF16),
        compiler_params=params(32),
        name="outgoing_product",
    )(x)


def incoming_kernel(x_ref, out_ref):
    blocks, tiles, _, rows, cols = x_ref.shape
    per = cols // rows
    rights = [x_ref[:, q, 1].reshape(blocks * rows, cols) for q in range(tiles)]
    right = jnp.concatenate(rights, axis=1)
    for p in range(tiles):
        left = x_ref[:, p, 0].reshape(blocks * rows, cols)
        product = dot(left, right, 0, 0).astype(BF16)
        for q in range(tiles):
            out_ref[p * per : (p + 1) * per, q] = product[:, q * cols : (q + 1) * cols].reshape(per, rows, cols)


def incoming(x):
    blocks, tiles, _, rows, cols = x.shape
    return pl.pallas_call(
        incoming_kernel,
        out_shape=jax.ShapeDtypeStruct((blocks, tiles, rows, cols), BF16),
        compiler_params=params(32),
        name="incoming_product",
    )(x)


def update_of(p_ref, weights):
    ch, rows, cols = p_ref.shape
    p = p_ref[...].astype(F32)
    mean = jnp.sum(p, 0) * (1.0 / ch)
    square = jnp.sum(p * p, 0) * (1.0 / ch)
    scale = lax.rsqrt(jnp.maximum(square - mean * mean, 0.0) + epsilon)
    columns = dot(weights, jnp.ones((ch, cols), BF16), 0, 0)
    by_row = jnp.swapaxes(p_ref[...], 0, 1)
    summed = dot(weights, jnp.concatenate([by_row[i] for i in range(rows)], 1), 0, 0)
    return [
        (summed[:, i * cols : (i + 1) * cols] - columns * mean[i : i + 1]) * scale[i : i + 1]
        for i in range(rows)
    ]


def middle_kernel(p_ref, pair_ref, gate_ref, whole_ref, gw_ref, gain_ref, mid_ref, gate2_ref, out_ref):
    ch, rows, cols = p_ref.shape
    updates = update_of(p_ref, whole_ref[4])
    mids = []
    for i in range(rows):
        lanes = slice(i * cols, (i + 1) * cols)
        mid = (pair_ref[:, lanes].astype(F32) + gate_ref[:, lanes] * updates[i]).astype(BF16)
        mid_ref[:, lanes] = mid
        mids.append(mid)
    mid = jnp.concatenate(mids, 1).astype(F32)
    centered = mid - jnp.sum(mid, 0, keepdims=True) * (1.0 / ch)
    var = jnp.sum(centered * centered, 0, keepdims=True) * (1.0 / ch)
    normed = (centered * lax.rsqrt(var + epsilon)).astype(BF16)
    parts = dot(whole_ref[:4].reshape(4 * ch, ch), normed, 1, 0)
    for s in range(2):
        value = parts[2 * s * ch : (2 * s + 1) * ch]
        gate = jnp.tanh(parts[(2 * s + 1) * ch : (2 * s + 2) * ch])
        out_ref[:, s] = stacked((value + value * gate).astype(BF16), rows)
    gate2_ref[...] = gate_of(normed, gw_ref, gain_ref, 1)


def middle_step(p, pair, gate, whole, gate_weight, in_gain):
    ch, rows, cols = p.shape
    return pl.pallas_call(
        middle_kernel,
        out_shape=(
            jax.ShapeDtypeStruct(pair.shape, BF16),
            jax.ShapeDtypeStruct(pair.shape, F32),
            jax.ShapeDtypeStruct((ch, 2, rows, cols), BF16),
        ),
        compiler_params=params(32),
        name="middle_step",
    )(p, pair, gate, whole, gate_weight, in_gain)


def last_kernel(p_ref, mid_ref, gate_ref, whole_ref, out_hbm, buffer, sem):
    ch, rows, cols = p_ref.shape
    parts = sem.shape[0]
    per = rows // parts
    updates = update_of(p_ref, whole_ref[5])
    copies = []
    for g in range(parts):
        group = slice(g * per, (g + 1) * per)
        for i in range(g * per, (g + 1) * per):
            lanes = slice(i * cols, (i + 1) * cols)
            out = mid_ref[:, lanes].astype(F32) + gate_ref[:, lanes] * updates[i]
            buffer[i] = out.astype(BF16).T
        copies.append(pltpu.make_async_copy(buffer.at[group], out_hbm.at[group], sem.at[g]))
        copies[-1].start()
    for copy in copies:
        copy.wait()


def last_step(p, mid, gate, whole):
    ch, rows, cols = p.shape
    out = (rows, cols, mid.shape[0])
    return pl.pallas_call(
        last_kernel,
        in_specs=[WHOLE] * 4,
        out_specs=pl.BlockSpec(memory_space=pl.ANY),
        out_shape=jax.ShapeDtypeStruct(out, BF16),
        scratch_shapes=[pltpu.VMEM(out, BF16), pltpu.SemaphoreType.DMA((4,))],
        compiler_params=params(32),
        name="last_step",
    )(p, mid, gate, whole)


def gather_chan(x):
    n = lax.axis_size("chan")
    me = lax.axis_index("chan")
    far = n * lax.axis_size("blk") // 2
    parts = [x]
    for k in range(1, n):
        step = k ^ far if k & 2 else k
        pairs = [(i, i ^ step) for i in range(2 * far)]
        parts.append(lax.ppermute(x, ("blk", "chan"), pairs))
    bit = 1
    while bit < n:
        swap = (me & bit) != 0
        parts = [jnp.where(swap, parts[k ^ bit], parts[k]) for k in range(n)]
        bit *= 2
    return jnp.stack(parts, -2)


def on_device(pair_rep, proj_weight, gate_weight, out_weight, in_gain, out_gain):
    rows, width, ch = pair_rep.shape
    tiles = lax.axis_size("chan")
    blocks = lax.axis_size("blk")
    share = proj_weight.shape[3]
    cols = width // tiles
    everywhere = ("blk", "chan")

    turned = jnp.transpose(proj_weight, (0, 1, 3, 2))
    halves = project(pair_rep, turned, in_gain)

    turned, out_weight, out_gain, gain, halves = lax.optimization_barrier(
        (turned, out_weight, out_gain, in_gain, halves)
    )
    later = (turned[1].astype(F32) * (0.5 * gain[1])).astype(BF16)
    scaled = (out_weight.astype(F32) * out_gain[:, :, None]).astype(BF16)
    whole = gather_chan(jnp.concatenate([later, scaled], 0))
    whole = whole.reshape(6, share * tiles, ch)
    own = lax.dynamic_slice_in_dim(pair_rep, lax.axis_index("chan") * cols, cols, 1)
    own, gate = first_gate(own, gate_weight, in_gain)

    halves = lax.all_to_all(halves, "blk", 0, 0, tiled=True)
    halves, whole, own, gate = lax.optimization_barrier((halves, whole, own, gate))
    product = outgoing(halves, tiles).reshape(blocks * tiles, rows, cols)
    product = lax.all_to_all(product, everywhere, 0, 0, tiled=True)
    mid, gate, halves = middle_step(product, own, gate, whole, gate_weight, in_gain)
    halves = lax.all_to_all(halves, everywhere, 0, 0, tiled=True)

    product = incoming(halves.reshape(blocks, tiles, 2, rows, cols)).reshape(blocks * tiles, rows, cols)
    product = lax.all_to_all(product, everywhere, 0, 0, tiled=True)
    return last_step(product, mid, gate, whole)


def solution(mesh):
    placed = (
        P("blk", None, None),
        P(None, None, None, "chan"),
        P(),
        P(None, "chan", None),
        P(),
        P(None, "chan"),
    )
    return jax.shard_map(
        on_device, mesh=mesh, in_specs=placed, out_specs=P("blk", "chan", None), check_vma=False
    )
```

```python
import jax
import jax.numpy as jnp
from jax import lax
from jax.experimental import pallas as pl
from jax.experimental.pallas import tpu as pltpu
from jax.sharding import PartitionSpec as P

epsilon = 1e-05
F32 = jnp.float32
BF16 = jnp.bfloat16
WHOLE = pl.BlockSpec(memory_space=pltpu.VMEM)


def params(mib):
    return pltpu.CompilerParams(vmem_limit_bytes=mib * 1024 * 1024)


def cost(flops, moved):
    return pl.CostEstimate(flops=flops, bytes_accessed=moved, transcendentals=0)


def dot(a, b, ca, cb):
    return lax.dot_general(a, b, (((ca,), (cb,)), ((), ())), preferred_element_type=F32)


def center_down(x):
    ch = x.shape[0]
    eye = lax.broadcasted_iota(jnp.int32, (ch, ch), 0) == lax.broadcasted_iota(jnp.int32, (ch, ch), 1)
    center = (jnp.where(eye, 1.0, 0.0) - 1.0 / ch).astype(BF16)
    centered = dot(center, x, 1, 0)
    rounded = centered.astype(BF16)
    var = dot(jnp.full((16, ch), 1.0 / ch, BF16), rounded * rounded, 1, 0)[:8]
    return centered, var


def stacked(x, rows):
    cols = x.shape[1] // rows
    return jnp.swapaxes(jnp.stack([x[:, i * cols : (i + 1) * cols] for i in range(rows)], 0), 0, 1)


def project_kernel(x_ref, w_ref, gain_ref, out_ref):
    rows, cols, ch = x_ref.shape
    share = out_ref.shape[0]
    weights = (w_ref[0].reshape(4 * share, ch).astype(F32) * gain_ref[0:1]).astype(BF16)
    centered, var = center_down(x_ref[...].reshape(rows * cols, ch).T)
    centered = centered.astype(BF16)
    scale = 0.5 * lax.rsqrt(var + epsilon)
    scale = jnp.concatenate([scale] * (share // scale.shape[0]), 0)
    for s in range(2):
        parts = dot(weights[2 * s * share : (2 * s + 2) * share], centered, 1, 0)
        value = parts[:share] * scale
        gate = jnp.tanh(parts[share:] * scale)
        out_ref[:, s] = stacked((value + value * gate).astype(BF16), rows)


def project(x, w, gain):
    rows, width, ch = x.shape
    share = w.shape[2]
    cols = width // 2
    return pl.pallas_call(
        project_kernel,
        grid=(width // cols,),
        in_specs=[
            pl.BlockSpec((rows, cols, ch), lambda t: (0, t, 0)),
            pl.BlockSpec((1, *w.shape[1:]), lambda t: (0, 0, 0, 0)),
            WHOLE,
        ],
        out_specs=pl.BlockSpec((share, 2, rows, cols), lambda t: (0, 0, 0, t)),
        out_shape=jax.ShapeDtypeStruct((share, 2, rows, width), BF16),
        compiler_params=params(60),
        name="project_rows",
    )(x, w, gain)


def norm_down(x):
    centered, var = center_down(x)
    return (centered * lax.rsqrt(var[:1] + epsilon)).astype(BF16)


def gate_of(normed, w_ref, gain_ref, s):
    w = (w_ref[s].astype(F32).T * (0.5 * gain_ref[s : s + 1])).astype(BF16)
    return 0.5 + 0.5 * jnp.tanh(dot(w, normed, 1, 0))


def first_gate_kernel(x_ref, w_ref, gain_ref, turned_ref, gate_ref):
    rows, cols, ch = x_ref.shape
    turned = jnp.concatenate([x_ref[i].T for i in range(rows)], 1)
    turned_ref[...] = turned
    gate_ref[...] = gate_of(norm_down(turned), w_ref, gain_ref, 0)


def first_gate(x, w, gain):
    rows, cols, ch = x.shape
    return pl.pallas_call(
        first_gate_kernel,
        out_shape=(
            jax.ShapeDtypeStruct((ch, rows * cols), BF16),
            jax.ShapeDtypeStruct((ch, rows * cols), F32),
        ),
        compiler_params=params(32),
        cost_estimate=cost(2 * rows * cols * ch * ch, 8 * rows * cols * ch),
        name="first_gate",
    )(x, w, gain)


def outgoing_kernel(x_ref, out_ref):
    blocks, _, rows, n = x_ref.shape
    tiles, cols = out_ref.shape[1], out_ref.shape[3]
    left = x_ref[:, 0].reshape(blocks * rows, n)
    right = x_ref[:, 1].reshape(blocks * rows, n)
    product = dot(left, right, 1, 1).astype(BF16)
    for q in range(tiles):
        out_ref[:, q] = product[:, q * cols : (q + 1) * cols].reshape(blocks, rows, cols)


def outgoing(x, tiles):
    blocks, _, rows, n = x.shape
    return pl.pallas_call(
        outgoing_kernel,
        out_shape=jax.ShapeDtypeStruct((blocks, tiles, rows, n // tiles), BF16),
        compiler_params=params(32),
        name="outgoing_product",
    )(x)


def incoming_kernel(x_ref, out_ref):
    blocks, tiles, _, rows, cols = x_ref.shape
    left, right = (
        jnp.concatenate([x_ref[:, q, s].reshape(blocks * rows, cols) for q in range(tiles)], 1) for s in range(2)
    )
    product = dot(left, right, 0, 0).astype(BF16)
    for q in range(tiles):
        out_ref[:, q] = product[:, q * cols : (q + 1) * cols].reshape(blocks, rows, cols)


def incoming(x):
    blocks, tiles, _, rows, cols = x.shape
    return pl.pallas_call(
        incoming_kernel,
        out_shape=jax.ShapeDtypeStruct((blocks, tiles, rows, cols), BF16),
        compiler_params=params(32),
        name="incoming_product",
    )(x)


def update_of(p_ref, weights):
    ch, rows, cols = p_ref.shape
    p = p_ref[...].astype(F32)
    mean = jnp.sum(p, 0) * (1.0 / ch)
    square = jnp.sum(p * p, 0) * (1.0 / ch)
    scale = lax.rsqrt(jnp.maximum(square - mean * mean, 0.0) + epsilon)
    columns = dot(weights, jnp.ones((ch, cols), BF16), 0, 0)
    by_row = jnp.swapaxes(p_ref[...], 0, 1)
    summed = dot(weights, jnp.concatenate([by_row[i] for i in range(rows)], 1), 0, 0)
    return [
        (summed[:, i * cols : (i + 1) * cols] - columns * mean[i : i + 1]) * scale[i : i + 1]
        for i in range(rows)
    ]


def middle_kernel(p_ref, pair_ref, gate_ref, whole_ref, gw_ref, gain_ref, mid_ref, gate2_ref, out_ref):
    ch, rows, cols = p_ref.shape
    updates = update_of(p_ref, whole_ref[4])
    mids = []
    for i in range(rows):
        lanes = slice(i * cols, (i + 1) * cols)
        mid = (pair_ref[:, lanes].astype(F32) + gate_ref[:, lanes] * updates[i]).astype(BF16)
        mid_ref[:, lanes] = mid
        mids.append(mid)
    mid = jnp.concatenate(mids, 1).astype(F32)
    centered = mid - jnp.sum(mid, 0, keepdims=True) * (1.0 / ch)
    var = jnp.sum(centered * centered, 0, keepdims=True) * (1.0 / ch)
    normed = (centered * lax.rsqrt(var + epsilon)).astype(BF16)
    parts = dot(whole_ref[:4].reshape(4 * ch, ch), normed, 1, 0)
    for s in range(2):
        value = parts[2 * s * ch : (2 * s + 1) * ch]
        gate = jnp.tanh(parts[(2 * s + 1) * ch : (2 * s + 2) * ch])
        out_ref[:, s] = stacked((value + value * gate).astype(BF16), rows)
    gate2_ref[...] = gate_of(normed, gw_ref, gain_ref, 1)


def middle_step(p, pair, gate, whole, gate_weight, in_gain):
    ch, rows, cols = p.shape
    return pl.pallas_call(
        middle_kernel,
        out_shape=(
            jax.ShapeDtypeStruct(pair.shape, BF16),
            jax.ShapeDtypeStruct(pair.shape, F32),
            jax.ShapeDtypeStruct((ch, 2, rows, cols), BF16),
        ),
        compiler_params=params(32),
        name="middle_step",
    )(p, pair, gate, whole, gate_weight, in_gain)


def last_kernel(p_ref, mid_ref, gate_ref, whole_ref, out_hbm, buffer, sem):
    ch, rows, cols = p_ref.shape
    parts = sem.shape[0]
    per = rows // parts
    updates = update_of(p_ref, whole_ref[5])
    copies = []
    for g in range(parts):
        group = slice(g * per, (g + 1) * per)
        for i in range(g * per, (g + 1) * per):
            lanes = slice(i * cols, (i + 1) * cols)
            out = mid_ref[:, lanes].astype(F32) + gate_ref[:, lanes] * updates[i]
            buffer[i] = out.astype(BF16).T
        copies.append(pltpu.make_async_copy(buffer.at[group], out_hbm.at[group], sem.at[g]))
        copies[-1].start()
    for copy in copies:
        copy.wait()


def last_step(p, mid, gate, whole):
    ch, rows, cols = p.shape
    out = (rows, cols, mid.shape[0])
    return pl.pallas_call(
        last_kernel,
        in_specs=[WHOLE] * 4,
        out_specs=pl.BlockSpec(memory_space=pl.ANY),
        out_shape=jax.ShapeDtypeStruct(out, BF16),
        scratch_shapes=[pltpu.VMEM(out, BF16), pltpu.SemaphoreType.DMA((4,))],
        compiler_params=params(32),
        name="last_step",
    )(p, mid, gate, whole)


def gather_chan(x):
    n = lax.axis_size("chan")
    me = lax.axis_index("chan")
    far = n * lax.axis_size("blk") // 2
    parts = [x]
    for k in range(1, n):
        step = k ^ far if k & 2 else k
        pairs = [(i, i ^ step) for i in range(2 * far)]
        parts.append(lax.ppermute(x, ("blk", "chan"), pairs))
    bit = 1
    while bit < n:
        swap = (me & bit) != 0
        parts = [jnp.where(swap, parts[k ^ bit], parts[k]) for k in range(n)]
        bit *= 2
    return jnp.stack(parts, -2)


def on_device(pair_rep, proj_weight, gate_weight, out_weight, in_gain, out_gain):
    rows, width, ch = pair_rep.shape
    tiles = lax.axis_size("chan")
    blocks = lax.axis_size("blk")
    share = proj_weight.shape[3]
    cols = width // tiles
    everywhere = ("blk", "chan")

    turned = jnp.transpose(proj_weight, (0, 1, 3, 2))
    halves = project(pair_rep, turned, in_gain)

    turned, out_weight, out_gain, gain, halves = lax.optimization_barrier(
        (turned, out_weight, out_gain, in_gain, halves)
    )
    later = (turned[1].astype(F32) * (0.5 * gain[1])).astype(BF16)
    scaled = (out_weight.astype(F32) * out_gain[:, :, None]).astype(BF16)
    whole = gather_chan(jnp.concatenate([later, scaled], 0))
    whole = whole.reshape(6, share * tiles, ch)
    own = lax.dynamic_slice_in_dim(pair_rep, lax.axis_index("chan") * cols, cols, 1)
    own, gate = first_gate(own, gate_weight, in_gain)

    halves = lax.all_to_all(halves, "blk", 0, 0, tiled=True)
    halves, whole, own, gate = lax.optimization_barrier((halves, whole, own, gate))
    product = outgoing(halves, tiles).reshape(blocks * tiles, rows, cols)
    product = lax.all_to_all(product, everywhere, 0, 0, tiled=True)
    mid, gate, halves = middle_step(product, own, gate, whole, gate_weight, in_gain)
    halves = lax.all_to_all(halves, everywhere, 0, 0, tiled=True)

    product = incoming(halves.reshape(blocks, tiles, 2, rows, cols)).reshape(blocks * tiles, rows, cols)
    product = lax.all_to_all(product, everywhere, 0, 0, tiled=True)
    return last_step(product, mid, gate, whole)


def solution(mesh):
    placed = (
        P("blk", None, None),
        P(None, None, None, "chan"),
        P(),
        P(None, "chan", None),
        P(),
        P(None, "chan"),
    )
    return jax.shard_map(
        on_device, mesh=mesh, in_specs=placed, out_specs=P("blk", "chan", None), check_vma=False
    )
```

```python
import jax
import jax.numpy as jnp
from jax import lax
from jax.experimental import pallas as pl
from jax.experimental.pallas import tpu as pltpu
from jax.sharding import PartitionSpec as P

epsilon = 1e-05
F32 = jnp.float32
BF16 = jnp.bfloat16
WHOLE = pl.BlockSpec(memory_space=pltpu.VMEM)


def params(mib):
    return pltpu.CompilerParams(vmem_limit_bytes=mib * 1024 * 1024)


def cost(flops, moved):
    return pl.CostEstimate(flops=flops, bytes_accessed=moved, transcendentals=0)


def dot(a, b, ca, cb):
    return lax.dot_general(a, b, (((ca,), (cb,)), ((), ())), preferred_element_type=F32)


def center_down(x):
    ch = x.shape[0]
    eye = lax.broadcasted_iota(jnp.int32, (ch, ch), 0) == lax.broadcasted_iota(jnp.int32, (ch, ch), 1)
    center = (jnp.where(eye, 1.0, 0.0) - 1.0 / ch).astype(BF16)
    centered = dot(center, x, 1, 0)
    rounded = centered.astype(BF16)
    var = dot(jnp.full((16, ch), 1.0 / ch, BF16), rounded * rounded, 1, 0)[:8]
    return centered, var


def stacked(x, rows):
    cols = x.shape[1] // rows
    return jnp.swapaxes(jnp.stack([x[:, i * cols : (i + 1) * cols] for i in range(rows)], 0), 0, 1)


def project_kernel(x_ref, w_ref, gain_ref, out_ref):
    rows, cols, ch = x_ref.shape
    share = out_ref.shape[0]
    weights = (w_ref[0].reshape(4 * share, ch).astype(F32) * gain_ref[0:1]).astype(BF16)
    centered, var = center_down(x_ref[...].reshape(rows * cols, ch).T)
    centered = centered.astype(BF16)
    scale = 0.5 * lax.rsqrt(var + epsilon)
    scale = jnp.concatenate([scale] * (share // scale.shape[0]), 0)
    for s in range(2):
        parts = dot(weights[2 * s * share : (2 * s + 2) * share], centered, 1, 0)
        value = parts[:share] * scale
        gate = jnp.tanh(parts[share:] * scale)
        out_ref[:, s] = stacked((value + value * gate).astype(BF16), rows)


def project(x, w, gain):
    rows, width, ch = x.shape
    share = w.shape[2]
    cols = width // 2
    return pl.pallas_call(
        project_kernel,
        grid=(width // cols,),
        in_specs=[
            pl.BlockSpec((rows, cols, ch), lambda t: (0, t, 0)),
            pl.BlockSpec((1, *w.shape[1:]), lambda t: (0, 0, 0, 0)),
            WHOLE,
        ],
        out_specs=pl.BlockSpec((share, 2, rows, cols), lambda t: (0, 0, 0, t)),
        out_shape=jax.ShapeDtypeStruct((share, 2, rows, width), BF16),
        compiler_params=params(60),
        name="project_rows",
    )(x, w, gain)


def norm_down(x):
    centered, var = center_down(x)
    return (centered * lax.rsqrt(var[:1] + epsilon)).astype(BF16)


def gate_of(normed, w_ref, gain_ref, s):
    w = (w_ref[s].astype(F32).T * (0.5 * gain_ref[s : s + 1])).astype(BF16)
    return 0.5 + 0.5 * jnp.tanh(dot(w, normed, 1, 0))


def first_gate_kernel(x_ref, w_ref, gain_ref, turned_ref, gate_ref):
    rows, cols, ch = x_ref.shape
    turned = jnp.concatenate([x_ref[i].T for i in range(rows)], 1)
    turned_ref[...] = turned
    gate_ref[...] = gate_of(norm_down(turned), w_ref, gain_ref, 0)


def first_gate(x, w, gain):
    rows, cols, ch = x.shape
    return pl.pallas_call(
        first_gate_kernel,
        out_shape=(
            jax.ShapeDtypeStruct((ch, rows * cols), BF16),
            jax.ShapeDtypeStruct((ch, rows * cols), F32),
        ),
        compiler_params=params(32),
        cost_estimate=cost(2 * rows * cols * ch * ch, 8 * rows * cols * ch),
        name="first_gate",
    )(x, w, gain)


def outgoing_kernel(x_ref, out_ref):
    blocks, _, rows, n = x_ref.shape
    tiles, cols = out_ref.shape[1], out_ref.shape[3]
    left = x_ref[:, 0].reshape(blocks * rows, n)
    right = x_ref[:, 1].reshape(blocks * rows, n)
    product = dot(left, right, 1, 1).astype(BF16)
    for q in range(tiles):
        out_ref[:, q] = product[:, q * cols : (q + 1) * cols].reshape(blocks, rows, cols)


def outgoing(x, tiles):
    blocks, _, rows, n = x.shape
    return pl.pallas_call(
        outgoing_kernel,
        out_shape=jax.ShapeDtypeStruct((blocks, tiles, rows, n // tiles), BF16),
        compiler_params=params(32),
        name="outgoing_product",
    )(x)


def incoming_kernel(x_ref, out_ref):
    blocks, tiles, _, rows, cols = x_ref.shape
    left, right = (
        jnp.concatenate([x_ref[:, q, s].reshape(blocks * rows, cols) for q in range(tiles)], 1) for s in range(2)
    )
    product = dot(left, right, 0, 0).astype(BF16)
    for q in range(tiles):
        out_ref[:, q] = product[:, q * cols : (q + 1) * cols].reshape(blocks, rows, cols)


def incoming(x):
    blocks, tiles, _, rows, cols = x.shape
    return pl.pallas_call(
        incoming_kernel,
        out_shape=jax.ShapeDtypeStruct((blocks, tiles, rows, cols), BF16),
        compiler_params=params(32),
        name="incoming_product",
    )(x)


def update_of(p_ref, weights):
    ch, rows, cols = p_ref.shape
    p = p_ref[...].astype(F32)
    mean = jnp.sum(p, 0) * (1.0 / ch)
    square = jnp.sum(p * p, 0) * (1.0 / ch)
    scale = lax.rsqrt(jnp.maximum(square - mean * mean, 0.0) + epsilon)
    columns = dot(weights, jnp.ones((ch, cols), BF16), 0, 0)
    by_row = jnp.swapaxes(p_ref[...], 0, 1)
    summed = dot(weights, jnp.concatenate([by_row[i] for i in range(rows)], 1), 0, 0)
    return [
        (summed[:, i * cols : (i + 1) * cols] - columns * mean[i : i + 1]) * scale[i : i + 1]
        for i in range(rows)
    ]


def middle_kernel(p_ref, pair_ref, gate_ref, whole_ref, gw_ref, gain_ref, mid_ref, gate2_ref, out_ref):
    ch, rows, cols = p_ref.shape
    updates = update_of(p_ref, whole_ref[4])
    mids = []
    for i in range(rows):
        lanes = slice(i * cols, (i + 1) * cols)
        mid = (pair_ref[:, lanes].astype(F32) + gate_ref[:, lanes] * updates[i]).astype(BF16)
        mid_ref[:, lanes] = mid
        mids.append(mid)
    mid = jnp.concatenate(mids, 1).astype(F32)
    centered = mid - jnp.sum(mid, 0, keepdims=True) * (1.0 / ch)
    var = jnp.sum(centered * centered, 0, keepdims=True) * (1.0 / ch)
    normed = (centered * lax.rsqrt(var + epsilon)).astype(BF16)
    parts = dot(whole_ref[:4].reshape(4 * ch, ch), normed, 1, 0)
    for s in range(2):
        value = parts[2 * s * ch : (2 * s + 1) * ch]
        gate = jnp.tanh(parts[(2 * s + 1) * ch : (2 * s + 2) * ch])
        out_ref[:, s] = stacked((value + value * gate).astype(BF16), rows)
    gate2_ref[...] = gate_of(normed, gw_ref, gain_ref, 1)


def middle_step(p, pair, gate, whole, gate_weight, in_gain):
    ch, rows, cols = p.shape
    return pl.pallas_call(
        middle_kernel,
        out_shape=(
            jax.ShapeDtypeStruct(pair.shape, BF16),
            jax.ShapeDtypeStruct(pair.shape, F32),
            jax.ShapeDtypeStruct((ch, 2, rows, cols), BF16),
        ),
        compiler_params=params(32),
        name="middle_step",
    )(p, pair, gate, whole, gate_weight, in_gain)


def last_kernel(p_ref, mid_ref, gate_ref, whole_ref, out_hbm, buffer, sem):
    ch, rows, cols = p_ref.shape
    parts = sem.shape[0]
    per = rows // parts
    updates = update_of(p_ref, whole_ref[5])
    copies = []
    for g in range(parts):
        group = slice(g * per, (g + 1) * per)
        lanes = slice(g * per * cols, (g + 1) * per * cols)
        update = jnp.concatenate(updates[group], 1)
        out = mid_ref[:, lanes].astype(F32) + gate_ref[:, lanes] * update
        buffer[group] = out.astype(BF16).T.reshape(per, cols, out.shape[0])
        copies.append(pltpu.make_async_copy(buffer.at[group], out_hbm.at[group], sem.at[g]))
        copies[-1].start()
    for copy in copies:
        copy.wait()


def last_step(p, mid, gate, whole):
    ch, rows, cols = p.shape
    out = (rows, cols, mid.shape[0])
    return pl.pallas_call(
        last_kernel,
        in_specs=[WHOLE] * 4,
        out_specs=pl.BlockSpec(memory_space=pl.ANY),
        out_shape=jax.ShapeDtypeStruct(out, BF16),
        scratch_shapes=[pltpu.VMEM(out, BF16), pltpu.SemaphoreType.DMA((4,))],
        compiler_params=params(32),
        name="last_step",
    )(p, mid, gate, whole)


def gather_chan(x):
    n = lax.axis_size("chan")
    me = lax.axis_index("chan")
    far = n * lax.axis_size("blk") // 2
    parts = [x]
    for k in range(1, n):
        step = k ^ far if k & 2 else k
        pairs = [(i, i ^ step) for i in range(2 * far)]
        parts.append(lax.ppermute(x, ("blk", "chan"), pairs))
    bit = 1
    while bit < n:
        swap = (me & bit) != 0
        parts = [jnp.where(swap, parts[k ^ bit], parts[k]) for k in range(n)]
        bit *= 2
    return jnp.stack(parts, -2)


def on_device(pair_rep, proj_weight, gate_weight, out_weight, in_gain, out_gain):
    rows, width, ch = pair_rep.shape
    tiles = lax.axis_size("chan")
    blocks = lax.axis_size("blk")
    share = proj_weight.shape[3]
    cols = width // tiles
    everywhere = ("blk", "chan")

    turned = jnp.transpose(proj_weight, (0, 1, 3, 2))
    halves = project(pair_rep, turned, in_gain)

    turned, out_weight, out_gain, gain, halves = lax.optimization_barrier(
        (turned, out_weight, out_gain, in_gain, halves)
    )
    later = (turned[1].astype(F32) * (0.5 * gain[1])).astype(BF16)
    scaled = (out_weight.astype(F32) * out_gain[:, :, None]).astype(BF16)
    whole = gather_chan(jnp.concatenate([later, scaled], 0))
    whole = whole.reshape(6, share * tiles, ch)
    own = lax.dynamic_slice_in_dim(pair_rep, lax.axis_index("chan") * cols, cols, 1)
    own, gate = first_gate(own, gate_weight, in_gain)

    halves = lax.all_to_all(halves, "blk", 0, 0, tiled=True)
    halves, whole, own, gate = lax.optimization_barrier((halves, whole, own, gate))
    product = outgoing(halves, tiles).reshape(blocks * tiles, rows, cols)
    product = lax.all_to_all(product, everywhere, 0, 0, tiled=True)
    mid, gate, halves = middle_step(product, own, gate, whole, gate_weight, in_gain)
    halves = lax.all_to_all(halves, everywhere, 0, 0, tiled=True)

    product = incoming(halves.reshape(blocks, tiles, 2, rows, cols)).reshape(blocks * tiles, rows, cols)
    product = lax.all_to_all(product, everywhere, 0, 0, tiled=True)
    return last_step(product, mid, gate, whole)


def solution(mesh):
    placed = (
        P("blk", None, None),
        P(None, None, None, "chan"),
        P(),
        P(None, "chan", None),
        P(),
        P(None, "chan"),
    )
    return jax.shard_map(
        on_device, mesh=mesh, in_specs=placed, out_specs=P("blk", "chan", None), check_vma=False
    )
```

```python
import jax
import jax.numpy as jnp
from jax import lax
from jax.experimental import pallas as pl
from jax.experimental.pallas import tpu as pltpu
from jax.sharding import PartitionSpec as P

epsilon = 1e-05
F32 = jnp.float32
BF16 = jnp.bfloat16
WHOLE = pl.BlockSpec(memory_space=pltpu.VMEM)


def params(mib):
    return pltpu.CompilerParams(vmem_limit_bytes=mib * 1024 * 1024)


def cost(flops, moved):
    return pl.CostEstimate(flops=flops, bytes_accessed=moved, transcendentals=0)


def dot(a, b, ca, cb):
    return lax.dot_general(a, b, (((ca,), (cb,)), ((), ())), preferred_element_type=F32)


def center_down(x):
    ch = x.shape[0]
    eye = lax.broadcasted_iota(jnp.int32, (ch, ch), 0) == lax.broadcasted_iota(jnp.int32, (ch, ch), 1)
    center = (jnp.where(eye, 1.0, 0.0) - 1.0 / ch).astype(BF16)
    centered = dot(center, x, 1, 0)
    rounded = centered.astype(BF16)
    var = dot(jnp.full((16, ch), 1.0 / ch, BF16), rounded * rounded, 1, 0)[:8]
    return centered, var


def stacked(x, rows):
    cols = x.shape[1] // rows
    return jnp.swapaxes(jnp.stack([x[:, i * cols : (i + 1) * cols] for i in range(rows)], 0), 0, 1)


def project_kernel(x_ref, w_ref, gain_ref, out_ref):
    rows, cols, ch = x_ref.shape
    share = out_ref.shape[0]
    weights = (w_ref[0].reshape(4 * share, ch).astype(F32) * gain_ref[0:1]).astype(BF16)
    centered, var = center_down(x_ref[...].reshape(rows * cols, ch).T)
    centered = centered.astype(BF16)
    scale = 0.5 * lax.rsqrt(var + epsilon)
    scale = jnp.concatenate([scale] * (share // scale.shape[0]), 0)
    for s in range(2):
        parts = dot(weights[2 * s * share : (2 * s + 2) * share], centered, 1, 0)
        value = parts[:share] * scale
        gate = jnp.tanh(parts[share:] * scale)
        out_ref[:, s] = stacked((value + value * gate).astype(BF16), rows)


def project(x, w, gain):
    rows, width, ch = x.shape
    share = w.shape[2]
    cols = width // 2
    return pl.pallas_call(
        project_kernel,
        grid=(width // cols,),
        in_specs=[
            pl.BlockSpec((rows, cols, ch), lambda t: (0, t, 0)),
            pl.BlockSpec((1, *w.shape[1:]), lambda t: (0, 0, 0, 0)),
            WHOLE,
        ],
        out_specs=pl.BlockSpec((share, 2, rows, cols), lambda t: (0, 0, 0, t)),
        out_shape=jax.ShapeDtypeStruct((share, 2, rows, width), BF16),
        compiler_params=params(60),
        name="project_rows",
    )(x, w, gain)


def norm_down(x):
    centered, var = center_down(x)
    return (centered * lax.rsqrt(var[:1] + epsilon)).astype(BF16)


def gate_of(normed, w_ref, gain_ref, s):
    w = (w_ref[s].astype(F32).T * (0.5 * gain_ref[s : s + 1])).astype(BF16)
    return 0.5 + 0.5 * jnp.tanh(dot(w, normed, 1, 0))


def first_gate_kernel(x_ref, w_ref, gain_ref, turned_ref, gate_ref):
    rows, cols, ch = x_ref.shape
    turned = jnp.concatenate([x_ref[i].T for i in range(rows)], 1)
    turned_ref[...] = turned
    gate_ref[...] = gate_of(norm_down(turned), w_ref, gain_ref, 0)


def first_gate(x, w, gain):
    rows, cols, ch = x.shape
    return pl.pallas_call(
        first_gate_kernel,
        out_shape=(
            jax.ShapeDtypeStruct((ch, rows * cols), BF16),
            jax.ShapeDtypeStruct((ch, rows * cols), F32),
        ),
        compiler_params=params(32),
        cost_estimate=cost(2 * rows * cols * ch * ch, 8 * rows * cols * ch),
        name="first_gate",
    )(x, w, gain)


def outgoing_kernel(x_ref, out_ref):
    blocks, _, rows, n = x_ref.shape
    tiles, cols = out_ref.shape[1], out_ref.shape[3]
    left = x_ref[:, 0].reshape(blocks * rows, n)
    right = x_ref[:, 1].reshape(blocks * rows, n)
    product = dot(left, right, 1, 1).astype(BF16)
    for q in range(tiles):
        out_ref[:, q] = product[:, q * cols : (q + 1) * cols].reshape(blocks, rows, cols)


def outgoing(x, tiles):
    blocks, _, rows, n = x.shape
    return pl.pallas_call(
        outgoing_kernel,
        out_shape=jax.ShapeDtypeStruct((blocks, tiles, rows, n // tiles), BF16),
        compiler_params=params(32),
        name="outgoing_product",
    )(x)


def incoming_kernel(x_ref, out_ref):
    blocks, tiles, _, rows, cols = x_ref.shape
    left, right = (
        jnp.concatenate([x_ref[:, q, s].reshape(blocks * rows, cols) for q in range(tiles)], 1) for s in range(2)
    )
    product = dot(left, right, 0, 0).astype(BF16)
    for q in range(tiles):
        out_ref[:, q] = product[:, q * cols : (q + 1) * cols].reshape(blocks, rows, cols)


def incoming(x):
    blocks, tiles, _, rows, cols = x.shape
    return pl.pallas_call(
        incoming_kernel,
        out_shape=jax.ShapeDtypeStruct((blocks, tiles, rows, cols), BF16),
        compiler_params=params(32),
        name="incoming_product",
    )(x)


def update_of(p_ref, weights):
    ch, rows, cols = p_ref.shape
    p = p_ref[...].astype(F32)
    mean = jnp.sum(p, 0) * (1.0 / ch)
    square = jnp.sum(p * p, 0) * (1.0 / ch)
    scale = lax.rsqrt(jnp.maximum(square - mean * mean, 0.0) + epsilon)
    columns = dot(weights, jnp.ones((ch, cols), BF16), 0, 0)
    by_row = jnp.swapaxes(p_ref[...], 0, 1)
    summed = dot(weights, jnp.concatenate([by_row[i] for i in range(rows)], 1), 0, 0)
    return [
        (summed[:, i * cols : (i + 1) * cols] - columns * mean[i : i + 1]) * scale[i : i + 1]
        for i in range(rows)
    ]


def middle_kernel(p_ref, pair_ref, gate_ref, whole_ref, gw_ref, gain_ref, mid_ref, gate2_ref, out_ref):
    ch, rows, cols = p_ref.shape
    updates = update_of(p_ref, whole_ref[4])
    mids = []
    for i in range(rows):
        lanes = slice(i * cols, (i + 1) * cols)
        mid = (pair_ref[:, lanes].astype(F32) + gate_ref[:, lanes] * updates[i]).astype(BF16)
        mid_ref[:, lanes] = mid
        mids.append(mid)
    mid = jnp.concatenate(mids, 1).astype(F32)
    centered = mid - jnp.sum(mid, 0, keepdims=True) * (1.0 / ch)
    var = jnp.sum(centered * centered, 0, keepdims=True) * (1.0 / ch)
    normed = (centered * lax.rsqrt(var + epsilon)).astype(BF16)
    parts = dot(whole_ref[:4].reshape(4 * ch, ch), normed, 1, 0)
    for s in range(2):
        value = parts[2 * s * ch : (2 * s + 1) * ch]
        gate = jnp.tanh(parts[(2 * s + 1) * ch : (2 * s + 2) * ch])
        out_ref[:, s] = stacked((value + value * gate).astype(BF16), rows)
    gate2_ref[...] = gate_of(normed, gw_ref, gain_ref, 1).astype(BF16)


def middle_step(p, pair, gate, whole, gate_weight, in_gain):
    ch, rows, cols = p.shape
    return pl.pallas_call(
        middle_kernel,
        out_shape=(
            jax.ShapeDtypeStruct(pair.shape, BF16),
            jax.ShapeDtypeStruct(pair.shape, BF16),
            jax.ShapeDtypeStruct((ch, 2, rows, cols), BF16),
        ),
        compiler_params=params(32),
        name="middle_step",
    )(p, pair, gate, whole, gate_weight, in_gain)


def last_kernel(p_ref, mid_ref, gate_ref, whole_ref, out_hbm, buffer, sem):
    ch, rows, cols = p_ref.shape
    parts = sem.shape[0]
    per = rows // parts
    updates = update_of(p_ref, whole_ref[5])
    copies = []
    for g in range(parts):
        group = slice(g * per, (g + 1) * per)
        for i in range(g * per, (g + 1) * per):
            lanes = slice(i * cols, (i + 1) * cols)
            out = mid_ref[:, lanes].astype(F32) + gate_ref[:, lanes].astype(F32) * updates[i]
            buffer[i] = out.astype(BF16).T
        copies.append(pltpu.make_async_copy(buffer.at[group], out_hbm.at[group], sem.at[g]))
        copies[-1].start()
    for copy in copies:
        copy.wait()


def last_step(p, mid, gate, whole):
    ch, rows, cols = p.shape
    out = (rows, cols, mid.shape[0])
    return pl.pallas_call(
        last_kernel,
        in_specs=[WHOLE] * 4,
        out_specs=pl.BlockSpec(memory_space=pl.ANY),
        out_shape=jax.ShapeDtypeStruct(out, BF16),
        scratch_shapes=[pltpu.VMEM(out, BF16), pltpu.SemaphoreType.DMA((4,))],
        compiler_params=params(32),
        name="last_step",
    )(p, mid, gate, whole)


def gather_chan(x):
    n = lax.axis_size("chan")
    me = lax.axis_index("chan")
    far = n * lax.axis_size("blk") // 2
    parts = [x]
    for k in range(1, n):
        step = k ^ far if k & 2 else k
        pairs = [(i, i ^ step) for i in range(2 * far)]
        parts.append(lax.ppermute(x, ("blk", "chan"), pairs))
    bit = 1
    while bit < n:
        swap = (me & bit) != 0
        parts = [jnp.where(swap, parts[k ^ bit], parts[k]) for k in range(n)]
        bit *= 2
    return jnp.stack(parts, -2)


def on_device(pair_rep, proj_weight, gate_weight, out_weight, in_gain, out_gain):
    rows, width, ch = pair_rep.shape
    tiles = lax.axis_size("chan")
    blocks = lax.axis_size("blk")
    share = proj_weight.shape[3]
    cols = width // tiles
    everywhere = ("blk", "chan")

    turned = jnp.transpose(proj_weight, (0, 1, 3, 2))
    halves = project(pair_rep, turned, in_gain)

    turned, out_weight, out_gain, gain, halves = lax.optimization_barrier(
        (turned, out_weight, out_gain, in_gain, halves)
    )
    later = (turned[1].astype(F32) * (0.5 * gain[1])).astype(BF16)
    scaled = (out_weight.astype(F32) * out_gain[:, :, None]).astype(BF16)
    whole = gather_chan(jnp.concatenate([later, scaled], 0))
    whole = whole.reshape(6, share * tiles, ch)
    own = lax.dynamic_slice_in_dim(pair_rep, lax.axis_index("chan") * cols, cols, 1)
    own, gate = first_gate(own, gate_weight, in_gain)

    halves = lax.all_to_all(halves, "blk", 0, 0, tiled=True)
    halves, whole, own, gate = lax.optimization_barrier((halves, whole, own, gate))
    product = outgoing(halves, tiles).reshape(blocks * tiles, rows, cols)
    product = lax.all_to_all(product, everywhere, 0, 0, tiled=True)
    mid, gate, halves = middle_step(product, own, gate, whole, gate_weight, in_gain)
    halves = lax.all_to_all(halves, everywhere, 0, 0, tiled=True)

    product = incoming(halves.reshape(blocks, tiles, 2, rows, cols)).reshape(blocks * tiles, rows, cols)
    product = lax.all_to_all(product, everywhere, 0, 0, tiled=True)
    return last_step(product, mid, gate, whole)


def solution(mesh):
    placed = (
        P("blk", None, None),
        P(None, None, None, "chan"),
        P(),
        P(None, "chan", None),
        P(),
        P(None, "chan"),
    )
    return jax.shard_map(
        on_device, mesh=mesh, in_specs=placed, out_specs=P("blk", "chan", None), check_vma=False
    )
```
